32 devices in a mesh: groups: 1, ctx: 16 (over z, y, x), head: 1, pair: 2 (over core).
Axes of the slice: x: 2, y: 2, z: 4, core: 2. Of those that a mesh axis runs over, the one named last changes fastest.
Arguments:
- queries: bfloat16 [8192, 3584], P(('groups', 'ctx', 'pair'), 'head'), may hold values from -80 to 80
- key_state_rows: bfloat16 [8192, 512], P(('groups', 'ctx', 'pair'), 'head'), may hold values from -8 to 8
- wanted: int32 [32, 31], P('groups'), may hold values from 0 to 127, as said below
- selected: int32 [128, 28, 16], P(('groups', 'ctx', 'pair'), 'head'), may hold values from 0 to 38, all different within a row
- w_query: bfloat16 [128, 128], replicated, may hold values from -0.5 to 0.5
- key_gate_weight: bfloat16 [384, 128], replicated, may hold values from -0.3125 to 0.3125
Outputs:
- distill_kl: float32 [128, 28], P(('groups', 'ctx', 'pair'), 'head')
The draws below stay inside these ranges and needn't reach their ends.
Inputs may be any that keep to these rules, and one draw needn't show every extreme that they name: `wanted`: row i names 31 different storage blocks, none held by storage spans i and i xor 1; they lie in 30 different spans, one span named twice, so that at most 2 come from any one span. `selected`: each query block and head lists 16 different candidate places.
All inputs are finite; a program needn't handle non-finite values.
Results may differ from the reference program's by a relative error of at most 0.00078.
Values may be sent and summed in bfloat16 or wider, within the bound.
No kernel may reach another device: no remote copies, remote signals or barrier semaphores. Data moves between devices by JAX's collectives and lax.ppermute only.
A program may use at most 64 MiB of HBM per device.

```python
import math
import jax
import jax.numpy as jnp
from jax import lax

QUERY_HEADS = 28
KEY_HEADS = 4
HEAD_SIZE = 128
GATE_WIDTH = 128
BLOCK_TOKENS = 64
NSEL = 16
SPAN = 256
REQ = 31
SEQUENCE_TOKENS = 8192
SEQUENCE_BLOCKS = 128
CANDIDATE_COUNT = 39


def key_field(key):
    random_noise_key = jax.random.fold_in(key, 11)
    random_shift_key = jax.random.fold_in(key, 12)
    noise_base = jnp.clip(jax.random.normal(random_noise_key, (SEQUENCE_TOKENS, KEY_HEADS * HEAD_SIZE), jnp.float32), -4.0, 4.0)
    shifted_block = jnp.clip(jax.random.normal(random_shift_key, (SEQUENCE_BLOCKS, 1, KEY_HEADS * HEAD_SIZE), jnp.float32), -4.0, 4.0)
    return (noise_base.reshape(SEQUENCE_BLOCKS, BLOCK_TOKENS, KEY_HEADS * HEAD_SIZE) + shifted_block).reshape(SEQUENCE_TOKENS, KEY_HEADS * HEAD_SIZE)


def query_field(key):
    random_noise_key = jax.random.fold_in(key, 21)
    random_shift_key = jax.random.fold_in(key, 22)
    noise_base = jnp.clip(jax.random.normal(random_noise_key, (SEQUENCE_TOKENS, QUERY_HEADS * HEAD_SIZE), jnp.float32), -4.0, 4.0)
    shifted_block = jnp.clip(jax.random.normal(random_shift_key, (SEQUENCE_BLOCKS, 1, QUERY_HEADS * HEAD_SIZE), jnp.float32), -4.0, 4.0)
    return (noise_base.reshape(SEQUENCE_BLOCKS, BLOCK_TOKENS, QUERY_HEADS * HEAD_SIZE) + shifted_block).reshape(SEQUENCE_TOKENS, QUERY_HEADS * HEAD_SIZE)


def draw_key_state_rows(key, part):
    return key_field(key).astype(jnp.bfloat16)


def draw_queries(key, part):
    field = query_field(key)
    return field.astype(jnp.bfloat16)


def draw_wanted(key, part):
    devices = SEQUENCE_TOKENS // SPAN
    span_count = SPAN // BLOCK_TOKENS

    def one_row(row_idx):
        row_key = jax.random.fold_in(key, row_idx)
        picked_rows = jax.random.permutation(jax.random.fold_in(row_key, 1), devices - 2)[:REQ - 1].astype(jnp.int32)
        pair_base = row_idx // 2 * 2
        holders = picked_rows + 2 * (picked_rows >= pair_base).astype(jnp.int32)
        holders = jnp.concatenate([holders, holders[:1]])
        spot_list = jax.random.randint(jax.random.fold_in(row_key, 2), (REQ,), 0, span_count).astype(jnp.int32)
        second = (spot_list[0] + jax.random.randint(jax.random.fold_in(row_key, 3), (), 1, span_count)) % span_count
        spot_list = jnp.concatenate([spot_list[:REQ - 1], second[None].astype(jnp.int32)])
        return (holders * span_count + spot_list).astype(jnp.int32)
    return jax.vmap(one_row)(jnp.arange(devices, dtype=jnp.int32))


def choose_distinct(rng, rows, amount, top, lift):
    order = jax.random.permutation(jax.random.fold_in(rng, 1), amount)
    pull = order
    for power in range(3):
        pull = pull * pull // amount
    pull = pull * lift // amount
    chance = jax.random.randint(jax.random.fold_in(rng, 2), (rows, amount), 0, 4096) + pull
    sure = jax.random.permutation(jax.random.fold_in(rng, 3), rows)[jnp.arange(amount) % rows]
    chance = jnp.where(jnp.arange(rows)[:, None] == sure[None, :], 1 << 14, chance)
    priority = chance * amount + jnp.arange(amount)
    return lax.top_k(priority.astype(jnp.int32), top)[1].astype(jnp.int32)


def centred(key, shape, scale, most, held_as=jnp.bfloat16):
    values = scale * jax.random.normal(key, shape, jnp.float32)
    return jnp.clip(values, min=-most, max=most).astype(held_as)


def setup_inputs(seed: int = 0, part: int = 0) -> dict:
    keys = jax.random.split(jax.random.key(seed), 7)
    own_keys = jax.random.split(jax.random.fold_in(keys[6], part), 7)
    return {
        "queries": draw_queries(jax.random.fold_in(jax.random.fold_in(keys[6], part), 71), part),
        "key_state_rows": draw_key_state_rows(jax.random.fold_in(jax.random.fold_in(keys[6], part), 71), part),
        "wanted": draw_wanted(jax.random.fold_in(jax.random.fold_in(keys[6], part), 71), part),
        "selected": choose_distinct(own_keys[3], SEQUENCE_BLOCKS * QUERY_HEADS, CANDIDATE_COUNT, NSEL, 0).reshape((SEQUENCE_BLOCKS, QUERY_HEADS, NSEL)),
        "w_query": centred(keys[4], (HEAD_SIZE, GATE_WIDTH), HEAD_SIZE ** -0.5, 0.5),
        "key_gate_weight": centred(keys[5], (3 * HEAD_SIZE, GATE_WIDTH), (3 * HEAD_SIZE) ** -0.5, 0.3125),
    }


def teacher_share(q_rows, candidate_keys, member, n_query, n_cand, query_group_width):
    score_scale = 1.0 / math.sqrt(q_rows.shape[2])

    def per_head(head_idx):
        q_head = lax.dynamic_index_in_dim(q_rows, head_idx, 1, keepdims=False)
        k_head = lax.dynamic_index_in_dim(candidate_keys, head_idx // query_group_width, 1, keepdims=False)
        chosen = lax.dynamic_index_in_dim(member, head_idx, 1, keepdims=False)
        scores = jnp.dot(q_head, k_head.T, preferred_element_type=jnp.float32) * score_scale
        scores = scores.reshape(n_query, BLOCK_TOKENS, n_cand, BLOCK_TOKENS)
        allowed = jnp.broadcast_to(chosen[:, None, :, None], scores.shape)
        row_max = lax.optimization_barrier(jnp.max(jnp.where(allowed, scores, -jnp.inf), axis=(2, 3), keepdims=True))
        weights = jnp.where(allowed, jnp.exp(scores - row_max), 0.0)
        row_total = lax.optimization_barrier(jnp.sum(weights, axis=(2, 3), keepdims=True))
        block_share = lax.optimization_barrier(jnp.sum(weights / row_total, axis=3))
        return lax.optimization_barrier(jnp.mean(block_share, axis=1))
    result = lax.map(per_head, jnp.arange(q_rows.shape[1], dtype=jnp.int32))
    return jnp.transpose(result, (1, 0, 2))

def pooling_keys(block_keys):
    key_max = lax.optimization_barrier(jnp.max(block_keys, axis=1))
    key_min = lax.optimization_barrier(jnp.min(block_keys, axis=1))
    key_mean = (lax.optimization_barrier(jnp.sum(block_keys.astype(jnp.float32), axis=1)) / BLOCK_TOKENS).astype(jnp.bfloat16)
    return jnp.concatenate([key_max, key_min, key_mean], axis=-1)

def key_projector(pooled, key_gate_weight):
    flat = pooled.reshape(-1, pooled.shape[-1])
    gate = jnp.dot(flat, key_gate_weight, preferred_element_type=jnp.float32).astype(jnp.bfloat16)
    return gate.reshape(pooled.shape[0], pooled.shape[1], key_gate_weight.shape[1])

def divergence(logits, teacher, candidate_index):
    row_max = lax.optimization_barrier(jnp.max(logits, axis=2, keepdims=True))
    row_total = lax.optimization_barrier(jnp.sum(jnp.exp(logits - row_max), axis=2, keepdims=True))
    log_gate = logits - row_max - jnp.log(row_total)
    picked = jnp.take(log_gate, candidate_index, axis=2)
    positive = teacher > 0
    safe_share = jnp.where(positive, teacher, 1.0)
    return lax.optimization_barrier(jnp.sum(jnp.where(positive, teacher * (jnp.log(safe_share) - picked), 0.0), axis=2))

def reference(queries, key_state_rows, wanted, selected, w_query, key_gate_weight):
    span_total = SEQUENCE_TOKENS // SPAN
    span_count = SPAN // BLOCK_TOKENS
    query_group_width = QUERY_HEADS // KEY_HEADS
    head_width = HEAD_SIZE
    block_keys = key_state_rows.reshape(SEQUENCE_BLOCKS, BLOCK_TOKENS, KEY_HEADS * HEAD_SIZE)
    key_gate_rows = key_projector(pooling_keys(block_keys.reshape(SEQUENCE_BLOCKS, BLOCK_TOKENS, KEY_HEADS, HEAD_SIZE)), key_gate_weight)
    local_ids = jnp.arange(span_count, dtype=jnp.int32)
    cand_range = jnp.arange(CANDIDATE_COUNT, dtype=jnp.int32)
    gate_scale = 1.0 / math.sqrt(GATE_WIDTH)

    def per_storage(span_idx):
        own_ids = (span_idx * span_count + local_ids).astype(jnp.int32)
        twin_ids = (jnp.bitwise_xor(span_idx, 1) * span_count + local_ids).astype(jnp.int32)
        wants = lax.dynamic_index_in_dim(wanted, span_idx, 0, keepdims=False).astype(jnp.int32)
        candidate_index = jnp.concatenate([own_ids, twin_ids, wants]).astype(jnp.int32)
        candidate_keys = block_keys[candidate_index].reshape(CANDIDATE_COUNT * BLOCK_TOKENS, KEY_HEADS, head_width)
        q_rows = lax.dynamic_slice_in_dim(queries, (span_idx * SPAN).astype(jnp.int32), SPAN, 0)
        q_rows = q_rows.reshape(SPAN, QUERY_HEADS, head_width)
        lists = lax.dynamic_slice_in_dim(selected, (span_idx * span_count).astype(jnp.int32), span_count, 0)
        member = jnp.any(lists[..., None] == cand_range, axis=2)
        member = member | (cand_range[None, None, :] == local_ids[:, None, None])
        teacher = teacher_share(q_rows, candidate_keys, member, span_count, CANDIDATE_COUNT, query_group_width)
        q_pool = (lax.optimization_barrier(jnp.sum(q_rows.reshape(span_count, BLOCK_TOKENS, QUERY_HEADS, head_width).astype(jnp.float32), axis=1)) / BLOCK_TOKENS).astype(jnp.bfloat16)
        query_gate_rows = jnp.dot(q_pool.reshape(-1, head_width), w_query, preferred_element_type=jnp.float32).astype(jnp.bfloat16)
        query_gate_rows = query_gate_rows.reshape(span_count, KEY_HEADS, query_group_width, GATE_WIDTH)
        logits = jnp.einsum('bkgd,jkd->bkgj', query_gate_rows.astype(jnp.float32), key_gate_rows.astype(jnp.float32)) * gate_scale
        logits = logits.reshape(span_count, QUERY_HEADS, SEQUENCE_BLOCKS)
        return divergence(logits, teacher, candidate_index)
    result = lax.map(per_storage, jnp.arange(span_total, dtype=jnp.int32))
    return result.reshape(SEQUENCE_BLOCKS, QUERY_HEADS)
```

```python
import functools
import math

import jax
import jax.numpy as jnp
from jax import lax
from jax.experimental import pallas as pl
from jax.experimental.pallas import tpu as pltpu
from jax.sharding import PartitionSpec as P

BLOCK = 64
LANES = 128
SEL_ROWS = 16
NEG = -1e37


def gate_kernel(dims, *refs):
    n_piece, n_key, heads, n_sel, n_cand, blocks, head_size = dims
    sel_s, cand_s, dup_s = refs[:3]
    q_in = refs[3 : 3 + n_piece]
    k_in = refs[3 + n_piece : 3 + n_piece + n_key]
    wq_ref, wk_ref, out_ref = refs[3 + n_piece + n_key : 6 + n_piece + n_key]
    qbuf, kbuf, pool, qpool, teach, ms, ss, lv, sem_q, sem_k = refs[6 + n_piece + n_key :]
    span = q_in[0].shape[0]
    span_blocks = span // BLOCK
    n_slot = n_sel + 1
    rows = n_piece * heads * span_blocks
    exp_scale = math.log2(math.e) / math.sqrt(head_size)

    q_copies = [
        pltpu.make_async_copy(q_in[i], qbuf.at[pl.ds(i * span, span)], sem_q.at[i]) for i in range(n_piece)
    ]
    k_rows = k_in[0].shape[0]
    k_copies = [
        pltpu.make_async_copy(k_in[i], kbuf.at[pl.ds(i * k_rows, k_rows)], sem_k.at[i]) for i in range(n_key)
    ]
    for copy in k_copies + q_copies:
        copy.start()
    ms[...] = jnp.full(ms.shape, NEG, jnp.float32)
    ss[...] = jnp.zeros(ss.shape, jnp.float32)
    lv[...] = jnp.full(lv.shape, -1, jnp.int32)
    for copy in k_copies + q_copies:
        copy.wait()

    def pool_step(i, carry):
        first = pl.multiple_of(i * 8 * BLOCK, 8 * BLOCK)
        keys = kbuf[pl.ds(first, 8 * BLOCK), :].astype(jnp.float32).reshape(8, BLOCK, head_size)
        at = pl.ds(pl.multiple_of(i * 8, 8), 8)
        pool[at, 0:head_size] = jnp.max(keys, axis=1)
        pool[at, head_size : 2 * head_size] = jnp.min(keys, axis=1)
        pool[at, 2 * head_size :] = jnp.sum(keys, axis=1) * (1.0 / BLOCK)
        return carry

    lax.fori_loop(0, blocks // 8, pool_step, 0)

    lane = lax.broadcasted_iota(jnp.int32, (1, LANES), 1)
    low = lane < BLOCK
    zeros = jnp.zeros((BLOCK, head_size), jnp.bfloat16)

    def pair_step(ph, t, u):
        piece = ph // heads
        head = ph - piece * heads
        q_at = pl.ds(pl.multiple_of(piece * span + t * 2 * BLOCK, 2 * BLOCK), 2 * BLOCK)
        q = qbuf[q_at, pl.ds(pl.multiple_of(head * head_size, head_size), head_size)]
        q0, q1 = q[:BLOCK], q[BLOCK:]
        row = ph * span_blocks + 2 * t
        means = [jnp.sum(x.astype(jnp.float32), axis=0, keepdims=True) * (1.0 / BLOCK) for x in (q0, q1)]
        qpool[pl.ds(row, 1), :] = means[0]
        qpool[pl.ds(row + 1, 1), :] = means[1]
        rhs = jnp.concatenate(
            [jnp.concatenate([q0, zeros], axis=1), jnp.concatenate([zeros, q1], axis=1)], axis=0
        )
        tiles = []
        for slot in range(n_slot):
            halves = []
            for half in range(2):
                if slot < n_sel:
                    place = sel_s[(row + half) * n_sel + slot]
                else:
                    place = 2 * t + half
                at = cand_s[piece * n_cand + place]
                lv[u, half, slot : slot + 1, :] = jnp.full((1, LANES), at, jnp.int32)
                halves.append(kbuf[pl.ds(pl.multiple_of(at * BLOCK, BLOCK), BLOCK), :])
            tiles.append(jnp.concatenate(halves, axis=1))
        scores = lax.dot_general(
            jnp.concatenate(tiles, axis=0),
            rhs,
            (((1,), (1,)), ((), ())),
            preferred_element_type=jnp.float32,
        )
        for slot in range(n_slot):
            part = scores[slot * BLOCK : (slot + 1) * BLOCK]
            top = jnp.max(part, axis=0, keepdims=True)
            total = jnp.sum(jnp.exp2((part - top) * exp_scale), axis=0, keepdims=True)
            if slot == n_sel:
                keep = jnp.where(low, 1 - dup_s[row], 1 - dup_s[row + 1])
                total = total * keep.astype(jnp.float32)
            ms[u, slot : slot + 1, :] = top
            ss[u, slot : slot + 1, :] = total
        tops = ms[u]
        weight = jnp.exp2((tops - jnp.max(tops, axis=0, keepdims=True)) * exp_scale) * ss[u]
        share = weight / jnp.sum(weight, axis=0, keepdims=True)
        for half in range(2):
            mine = low if half == 0 else jnp.logical_not(low)
            mean = jnp.sum(jnp.where(mine, share, 0.0), axis=1, keepdims=True) * (1.0 / BLOCK)
            for c in range(blocks // LANES):
                hit = lv[u, half] == lane + c * LANES
                teach[c, pl.ds(row + half, 1), :] = jnp.sum(
                    jnp.where(hit, mean, 0.0), axis=0, keepdims=True
                )

    def head_step(ph, carry):
        for t in range(span_blocks // 2):
            pair_step(ph, t, t)
        return carry

    lax.fori_loop(0, n_piece * heads, head_step, 0)

    k_gate = jnp.dot(
        pool[...].astype(jnp.bfloat16), wk_ref[...], preferred_element_type=jnp.float32
    ).astype(jnp.bfloat16)
    q_gate = jnp.dot(
        qpool[...].astype(jnp.bfloat16), wq_ref[...], preferred_element_type=jnp.float32
    ).astype(jnp.bfloat16)
    logits = lax.dot_general(
        q_gate, k_gate, (((1,), (1,)), ((), ())), preferred_element_type=jnp.float32
    ) * (1.0 / math.sqrt(wq_ref.shape[1]))
    top = jnp.max(logits, axis=1, keepdims=True)
    log_gate = logits - top - jnp.log(jnp.sum(jnp.exp(logits - top), axis=1, keepdims=True))
    teacher = jnp.concatenate([teach[c] for c in range(blocks // LANES)], axis=1)
    positive = teacher > 0
    safe = jnp.where(positive, teacher, 1.0)
    out_ref[...] = jnp.sum(
        jnp.where(positive, teacher * (jnp.log(safe) - log_gate), 0.0), axis=1, keepdims=True
    )


def gate_call(sel, cand, dup, q_pieces, k_pieces, w_query, key_gate_weight, heads, n_sel, n_cand):
    head_size = w_query.shape[0]
    span = q_pieces[0].shape[0]
    k_rows = k_pieces[0].shape[0]
    blocks = len(k_pieces) * k_rows // BLOCK
    rows = len(q_pieces) * heads * (span // BLOCK)
    dims = (len(q_pieces), len(k_pieces), heads, n_sel, n_cand, blocks, head_size)
    unroll = span // BLOCK // 2
    slots = -(-(n_sel + 1) // 8) * 8
    smem = pl.BlockSpec(memory_space=pltpu.SMEM)
    hbm = pl.BlockSpec(memory_space=pl.ANY)
    vmem = pl.BlockSpec(memory_space=pltpu.VMEM)
    return pl.pallas_call(
        functools.partial(gate_kernel, dims),
        out_shape=jax.ShapeDtypeStruct((rows, 1), jnp.float32),
        in_specs=[smem] * 3 + [hbm] * (len(q_pieces) + len(k_pieces)) + [vmem] * 2,
        out_specs=vmem,
        scratch_shapes=[
            pltpu.VMEM((len(q_pieces) * span, heads * head_size), jnp.bfloat16),
            pltpu.VMEM((blocks * BLOCK, head_size), jnp.bfloat16),
            pltpu.VMEM((blocks, 3 * head_size), jnp.float32),
            pltpu.VMEM((rows, head_size), jnp.float32),
            pltpu.VMEM((blocks // LANES, rows, LANES), jnp.float32),
            pltpu.VMEM((unroll, slots, LANES), jnp.float32),
            pltpu.VMEM((unroll, slots, LANES), jnp.float32),
            pltpu.VMEM((unroll, 2, slots, LANES), jnp.int32),
            pltpu.SemaphoreType.DMA((len(q_pieces),)),
            pltpu.SemaphoreType.DMA((len(k_pieces),)),
        ],
        compiler_params=pltpu.CompilerParams(vmem_limit_bytes=40 * 1024 * 1024),
    )(sel, cand, dup, *q_pieces, *k_pieces, w_query, key_gate_weight)


def per_device(queries, key_state_rows, wanted, selected, w_query, key_gate_weight):
    n_ctx, n_pair = lax.axis_size("ctx"), lax.axis_size("pair")
    ctx, core = lax.axis_index("ctx"), lax.axis_index("pair")
    head_size = w_query.shape[0]
    span, key_width = key_state_rows.shape
    span_blocks = span // BLOCK
    q_heads = queries.shape[1] // head_size
    kv_heads = key_width // head_size
    heads = q_heads // kv_heads
    n_sel = selected.shape[2]
    plane = kv_heads if kv_heads in (1, 2, 4) and n_ctx % kv_heads == 0 and n_pair == 2 else 1
    layers = n_ctx // plane
    ring = plane > 1 and layers <= 4
    spot = ctx % plane
    layer = ctx // plane

    def place_of(block):
        if not ring:
            return block
        span_id = block // span_blocks
        other_ctx = span_id // n_pair
        step = (layer - other_ctx // plane) % layers
        which = (other_ctx % plane) ^ spot
        side = (span_id % n_pair) ^ core
        return ((side * layers + step) * plane + which) * span_blocks + block % span_blocks

    local_ids = jnp.arange(span_blocks, dtype=jnp.int32)
    candidates = []
    for p in range(plane if ring else 1):
        other_span = (ctx ^ p) * n_pair + core
        wants = lax.dynamic_index_in_dim(wanted, other_span, 0, keepdims=False)
        candidates.append(
            jnp.concatenate(
                [other_span * span_blocks + local_ids, (other_span ^ 1) * span_blocks + local_ids, wants]
            )
        )
    n_cand = candidates[0].shape[0]
    cand = place_of(jnp.stack(candidates)).astype(jnp.int32).reshape(-1)

    def lists(sel):
        sel = jnp.transpose(sel, (0, 2, 1, 3))
        dup = jnp.any(sel == local_ids[None, None, :, None], axis=3).astype(jnp.int32)
        return sel.reshape(-1), dup.reshape(-1)

    if not ring:
        gathered = lax.all_gather(key_state_rows, ("ctx", "pair"), axis=0, tiled=True)
        outs = []
        for g in range(kv_heads):
            sel, dup = lists(selected[None, :, g * heads : (g + 1) * heads])
            out = gate_call(
                sel, cand, dup,
                [queries[:, g * heads * head_size : (g + 1) * heads * head_size]],
                [gathered[:, g * head_size : (g + 1) * head_size]],
                w_query, key_gate_weight, heads, n_sel, n_cand,
            )
            outs.append(jnp.transpose(out.reshape(heads, span_blocks)))
        return jnp.concatenate(outs, axis=1)

    def flipped(x, p):
        return x if p == 0 else lax.ppermute(x, "ctx", [(i, i ^ p) for i in range(n_ctx)])

    def other_core(x):
        return lax.ppermute(x, "pair", [(0, 1), (1, 0)])

    keys = [
        flipped(lax.dynamic_slice_in_dim(key_state_rows, (spot ^ p) * head_size, head_size, 1), p)
        for p in range(plane)
    ]
    steps = [jnp.concatenate(keys, axis=0)]
    sel_rows = jnp.pad(
        selected.astype(jnp.bfloat16),
        ((0, SEL_ROWS - span_blocks), (0, 0), (0, head_size - n_sel)),
    ).reshape(SEL_ROWS, q_heads * head_size)
    sent = jnp.concatenate([queries, sel_rows], axis=0)
    width = heads * head_size
    pieces = [
        flipped(lax.dynamic_slice_in_dim(sent, (spot ^ p) * width, width, 1), p) for p in range(plane)
    ]
    for _ in range(layers - 1):
        steps.append(
            lax.ppermute(steps[-1], "ctx", [(i, (i + plane) % n_ctx) for i in range(n_ctx)])
        )
    k_pieces = steps + [other_core(x) for x in steps]
    sel = jnp.stack([x[span : span + span_blocks] for x in pieces])
    sel = sel.reshape(plane, span_blocks, heads, head_size)[..., :n_sel].astype(jnp.int32)
    sel, dup = lists(sel)
    q_pieces = [x[:span] for x in pieces]
    out = gate_call(sel, cand, dup, q_pieces, k_pieces, w_query, key_gate_weight, heads, n_sel, n_cand)
    out = out.reshape(plane, heads, span_blocks)
    back = jnp.stack([flipped(out[p], p) for p in range(plane)])
    order = jnp.arange(plane, dtype=jnp.int32) ^ spot
    back = jnp.transpose(back[order], (2, 0, 1))
    return back.reshape(span_blocks, q_heads)


def solution(mesh):
    return jax.shard_map(
        per_device,
        mesh=mesh,
        in_specs=(
            P(("groups", "ctx", "pair"), "head"),
            P(("groups", "ctx", "pair"), "head"),
            P("groups", None),
            P(("groups", "ctx", "pair"), "head", None),
            P(),
            P(),
        ),
        out_specs=P(("groups", "ctx", "pair"), "head"),
        check_vma=False,
    )
```

```python
import functools
import math

import jax
import jax.numpy as jnp
from jax import lax
from jax.experimental import pallas as pl
from jax.experimental.pallas import tpu as pltpu
from jax.sharding import PartitionSpec as P

BLOCK = 64
LANES = 128
SEL_ROWS = 16
NEG = -1e37


def gate_kernel(dims, *refs):
    n_piece, n_key, heads, n_sel, n_cand, blocks, head_size = dims
    cand_s = refs[0]
    q_in = refs[1 : 1 + n_piece]
    k_in = refs[1 + n_piece : 1 + n_piece + n_key]
    refs = refs[1 + n_piece + n_key :]
    wq_ref, wk_ref = refs[:2]
    out_refs = refs[2 : 2 + n_piece]
    qbuf, kbuf, pool, qpool, teach, ms, ss, lv, sel_v, sel_s, sem_q, sem_k, sem_s = refs[2 + n_piece :]
    stride = q_in[0].shape[0]
    span = stride - SEL_ROWS
    span_blocks = span // BLOCK
    n_slot = n_sel + 1
    rows = n_piece * heads * span_blocks
    exp_scale = math.log2(math.e) / math.sqrt(head_size)

    q_copies = [
        pltpu.make_async_copy(q_in[i], qbuf.at[pl.ds(i * stride, stride)], sem_q.at[i]) for i in range(n_piece)
    ]
    k_rows = k_in[0].shape[0]
    k_copies = [
        pltpu.make_async_copy(k_in[i], kbuf.at[pl.ds(i * k_rows, k_rows)], sem_k.at[i]) for i in range(n_key)
    ]
    for copy in q_copies + k_copies:
        copy.start()
    ms[...] = jnp.full(ms.shape, NEG, jnp.float32)
    ss[...] = jnp.zeros(ss.shape, jnp.float32)
    lv[...] = jnp.full(lv.shape, -1, jnp.int32)
    for copy in q_copies:
        copy.wait()

    lane = lax.broadcasted_iota(jnp.int32, (1, LANES), 1)
    sub = lax.broadcasted_iota(jnp.int32, (SEL_ROWS, 1), 0)
    for i in range(n_piece):
        for h in range(heads):
            at = slice(h * head_size, h * head_size + LANES)
            mine = qbuf[i * stride + span : (i + 1) * stride, at].astype(jnp.int32)
            own = jnp.where((mine == sub) & (lane < n_sel), 1, 0)
            own = jnp.max(own, axis=1, keepdims=True)
            sel_v[i, :, h * LANES : (h + 1) * LANES] = jnp.where(lane == n_sel, own, mine)
    sel_copy = pltpu.make_async_copy(sel_v, sel_s, sem_s)
    sel_copy.start()
    for copy in k_copies:
        copy.wait()

    def pool_step(i, carry):
        first = pl.multiple_of(i * 8 * BLOCK, 8 * BLOCK)
        keys = kbuf[pl.ds(first, 8 * BLOCK), :].astype(jnp.float32).reshape(8, BLOCK, head_size)
        at = pl.ds(pl.multiple_of(i * 8, 8), 8)
        pool[at, 0:head_size] = jnp.max(keys, axis=1)
        pool[at, head_size : 2 * head_size] = jnp.min(keys, axis=1)
        pool[at, 2 * head_size :] = jnp.sum(keys, axis=1) * (1.0 / BLOCK)
        return carry

    lax.fori_loop(0, blocks // 8, pool_step, 0)
    sel_copy.wait()

    low = lane < BLOCK
    zeros = jnp.zeros((BLOCK, head_size), jnp.bfloat16)

    def pair_step(ph, t, u):
        piece = ph // heads
        head = ph - piece * heads
        q_at = pl.ds(pl.multiple_of(piece * stride + t * 2 * BLOCK, SEL_ROWS), 2 * BLOCK)
        q = qbuf[q_at, pl.ds(pl.multiple_of(head * head_size, head_size), head_size)]
        q0, q1 = q[:BLOCK], q[BLOCK:]
        row = ph * span_blocks + 2 * t
        means = [jnp.sum(x.astype(jnp.float32), axis=0, keepdims=True) * (1.0 / BLOCK) for x in (q0, q1)]
        qpool[pl.ds(row, 1), :] = means[0]
        qpool[pl.ds(row + 1, 1), :] = means[1]
        rhs = jnp.concatenate(
            [jnp.concatenate([q0, zeros], axis=1), jnp.concatenate([zeros, q1], axis=1)], axis=0
        )
        tiles = []
        for slot in range(n_slot):
            halves = []
            for half in range(2):
                if slot < n_sel:
                    place = sel_s[piece, 2 * t + half, head * LANES + slot]
                else:
                    place = 2 * t + half
                at = cand_s[piece * n_cand + place]
                lv[u, half, slot : slot + 1, :] = jnp.full((1, LANES), at, jnp.int32)
                halves.append(kbuf[pl.ds(pl.multiple_of(at * BLOCK, BLOCK), BLOCK), :])
            tiles.append(jnp.concatenate(halves, axis=1))
        scores = lax.dot_general(
            jnp.concatenate(tiles, axis=0),
            rhs,
            (((1,), (1,)), ((), ())),
            preferred_element_type=jnp.float32,
        )
        for slot in range(n_slot):
            part = scores[slot * BLOCK : (slot + 1) * BLOCK]
            top = jnp.max(part, axis=0, keepdims=True)
            total = jnp.sum(jnp.exp2((part - top) * exp_scale), axis=0, keepdims=True)
            if slot == n_sel:
                drop = [sel_s[piece, 2 * t + half, head * LANES + n_sel] for half in range(2)]
                total = total * (1 - jnp.where(low, drop[0], drop[1])).astype(jnp.float32)
            ms[u, slot : slot + 1, :] = top
            ss[u, slot : slot + 1, :] = total
        tops = ms[u]
        weight = jnp.exp2((tops - jnp.max(tops, axis=0, keepdims=True)) * exp_scale) * ss[u]
        share = weight / jnp.sum(weight, axis=0, keepdims=True)
        for half in range(2):
            mine = low if half == 0 else jnp.logical_not(low)
            mean = jnp.sum(jnp.where(mine, share, 0.0), axis=1, keepdims=True) * (1.0 / BLOCK)
            for c in range(blocks // LANES):
                hit = lv[u, half] == lane + c * LANES
                teach[c, pl.ds(row + half, 1), :] = jnp.sum(
                    jnp.where(hit, mean, 0.0), axis=0, keepdims=True
                )

    def head_step(ph, carry):
        for t in range(span_blocks // 2):
            pair_step(ph, t, t)
        return carry

    lax.fori_loop(0, n_piece * heads, head_step, 0)

    k_gate = jnp.dot(
        pool[...].astype(jnp.bfloat16), wk_ref[...], preferred_element_type=jnp.float32
    ).astype(jnp.bfloat16)
    q_gate = jnp.dot(
        qpool[...].astype(jnp.bfloat16), wq_ref[...], preferred_element_type=jnp.float32
    ).astype(jnp.bfloat16)
    logits = lax.dot_general(
        q_gate, k_gate, (((1,), (1,)), ((), ())), preferred_element_type=jnp.float32
    ) * (1.0 / math.sqrt(wq_ref.shape[1]))
    top = jnp.max(logits, axis=1, keepdims=True)
    log_gate = logits - top - jnp.log(jnp.sum(jnp.exp(logits - top), axis=1, keepdims=True))
    teacher = jnp.concatenate([teach[c] for c in range(blocks // LANES)], axis=1)
    positive = teacher > 0
    safe = jnp.where(positive, teacher, 1.0)
    kl = jnp.sum(jnp.where(positive, teacher * (jnp.log(safe) - log_gate), 0.0), axis=1, keepdims=True)
    r = lax.broadcasted_iota(jnp.int32, (rows, 1), 0)
    spread = jnp.where(r // span_blocks % heads == lane, kl, 0.0)
    r = lax.broadcasted_iota(jnp.int32, (1, rows), 1)
    b = lax.broadcasted_iota(jnp.int32, (8, 1), 0)
    for i in range(n_piece):
        pick = (r % span_blocks == b) & (r // (span_blocks * heads) == i) & (b < span_blocks)
        tile = jnp.dot(
            pick.astype(jnp.float32), spread, preferred_element_type=jnp.float32, precision=lax.Precision.HIGHEST
        )
        out_refs[i][...] = tile


def gate_call(cand, q_pieces, k_pieces, w_query, key_gate_weight, heads, n_sel, n_cand):
    head_size = w_query.shape[0]
    stride = q_pieces[0].shape[0]
    span_blocks = (stride - SEL_ROWS) // BLOCK
    n_piece = len(q_pieces)
    blocks = len(k_pieces) * k_pieces[0].shape[0] // BLOCK
    rows = n_piece * heads * span_blocks
    dims = (n_piece, len(k_pieces), heads, n_sel, n_cand, blocks, head_size)
    unroll = span_blocks // 2
    slots = -(-(n_sel + 1) // 8) * 8
    smem = pl.BlockSpec(memory_space=pltpu.SMEM)
    hbm = pl.BlockSpec(memory_space=pl.ANY)
    vmem = pl.BlockSpec(memory_space=pltpu.VMEM)
    return pl.pallas_call(
        functools.partial(gate_kernel, dims),
        out_shape=[jax.ShapeDtypeStruct((8, LANES), jnp.float32)] * n_piece,
        in_specs=[smem] + [hbm] * (n_piece + len(k_pieces)) + [vmem] * 2,
        out_specs=[vmem] * n_piece,
        scratch_shapes=[
            pltpu.VMEM((n_piece * stride, heads * head_size), jnp.bfloat16),
            pltpu.VMEM((blocks * BLOCK, head_size), jnp.bfloat16),
            pltpu.VMEM((blocks, 3 * head_size), jnp.float32),
            pltpu.VMEM((rows, head_size), jnp.float32),
            pltpu.VMEM((blocks // LANES, rows, LANES), jnp.float32),
            pltpu.VMEM((unroll, slots, LANES), jnp.float32),
            pltpu.VMEM((unroll, slots, LANES), jnp.float32),
            pltpu.VMEM((unroll, 2, slots, LANES), jnp.int32),
            pltpu.VMEM((n_piece, SEL_ROWS, heads * LANES), jnp.int32),
            pltpu.SMEM((n_piece, SEL_ROWS, heads * LANES), jnp.int32),
            pltpu.SemaphoreType.DMA((n_piece,)),
            pltpu.SemaphoreType.DMA((len(k_pieces),)),
            pltpu.SemaphoreType.DMA(()),
        ],
        compiler_params=pltpu.CompilerParams(vmem_limit_bytes=40 * 1024 * 1024),
    )(cand, *q_pieces, *k_pieces, w_query, key_gate_weight)


def per_device(queries, key_state_rows, wanted, selected, w_query, key_gate_weight):
    n_ctx, n_pair = lax.axis_size("ctx"), lax.axis_size("pair")
    ctx, core = lax.axis_index("ctx"), lax.axis_index("pair")
    head_size = w_query.shape[0]
    span, key_width = key_state_rows.shape
    span_blocks = span // BLOCK
    q_heads = queries.shape[1] // head_size
    kv_heads = key_width // head_size
    heads = q_heads // kv_heads
    n_sel = selected.shape[2]
    plane = kv_heads if kv_heads in (1, 2, 4) and n_ctx % kv_heads == 0 and n_pair == 2 else 1
    layers = n_ctx // plane
    ring = plane > 1 and layers <= 4
    spot = ctx % plane
    layer = ctx // plane

    def place_of(block):
        if not ring:
            return block
        span_id = block // span_blocks
        other_ctx = span_id // n_pair
        step = (layer - other_ctx // plane) % layers
        which = (other_ctx % plane) ^ spot
        side = (span_id % n_pair) ^ core
        return ((side * layers + step) * plane + which) * span_blocks + block % span_blocks

    local_ids = jnp.arange(span_blocks, dtype=jnp.int32)
    candidates = []
    for p in range(plane if ring else 1):
        other_span = (ctx ^ p) * n_pair + core
        wants = lax.dynamic_index_in_dim(wanted, other_span, 0, keepdims=False)
        candidates.append(
            jnp.concatenate(
                [other_span * span_blocks + local_ids, (other_span ^ 1) * span_blocks + local_ids, wants]
            )
        )
    n_cand = candidates[0].shape[0]
    cand = place_of(jnp.stack(candidates)).astype(jnp.int32).reshape(-1)

    sel_rows = jnp.pad(
        selected.astype(jnp.bfloat16),
        ((0, SEL_ROWS - span_blocks), (0, 0), (0, head_size - n_sel)),
    ).reshape(SEL_ROWS, q_heads * head_size)
    sent = jnp.concatenate([queries, sel_rows], axis=0)
    width = heads * head_size

    if not ring:
        gathered = lax.all_gather(key_state_rows, ("ctx", "pair"), axis=0, tiled=True)
        outs = []
        for g in range(kv_heads):
            (out,) = gate_call(
                cand,
                [sent[:, g * width : (g + 1) * width]],
                [gathered[:, g * head_size : (g + 1) * head_size]],
                w_query, key_gate_weight, heads, n_sel, n_cand,
            )
            outs.append(out[:span_blocks, :heads])
        return jnp.concatenate(outs, axis=1)

    def flipped(x, p):
        return x if p == 0 else lax.ppermute(x, "ctx", [(i, i ^ p) for i in range(n_ctx)])

    def other_core(x):
        return lax.ppermute(x, "pair", [(0, 1), (1, 0)])

    keys = [
        flipped(lax.dynamic_slice_in_dim(key_state_rows, (spot ^ p) * head_size, head_size, 1), p)
        for p in range(plane)
    ]
    parts = [lax.dynamic_slice_in_dim(sent, (spot ^ p) * width, width, 1) for p in range(plane)]
    steps = [jnp.concatenate(keys, axis=0)]
    steps[0], parts = lax.optimization_barrier((steps[0], parts))
    pieces = [flipped(x, p) for p, x in enumerate(parts)]
    for i in range(layers - 1):
        if i == 2:
            steps[2], pieces[1:3] = lax.optimization_barrier((steps[2], pieces[1:3]))
        steps.append(
            lax.ppermute(steps[-1], "ctx", [(i, (i + plane) % n_ctx) for i in range(n_ctx)])
        )
    k_pieces = steps + [other_core(x) for x in steps]
    outs = gate_call(cand, pieces, k_pieces, w_query, key_gate_weight, heads, n_sel, n_cand)
    back = [flipped(x, p)[:span_blocks, :heads] for p, x in enumerate(outs)]
    columns = []
    for g in range(plane):
        column = back[0]
        for p in range(1, plane):
            column = jnp.where(spot ^ g == p, back[p], column)
        columns.append(column)
    return jnp.concatenate(columns, axis=1)


def solution(mesh):
    return jax.shard_map(
        per_device,
        mesh=mesh,
        in_specs=(
            P(("groups", "ctx", "pair"), "head"),
            P(("groups", "ctx", "pair"), "head"),
            P("groups", None),
            P(("groups", "ctx", "pair"), "head", None),
            P(),
            P(),
        ),
        out_specs=P(("groups", "ctx", "pair"), "head"),
        check_vma=False,
    )
```

```python
import functools
import math

import jax
import jax.numpy as jnp
from jax import lax
from jax.experimental import pallas as pl
from jax.experimental.pallas import tpu as pltpu
from jax.sharding import PartitionSpec as P

BLOCK = 64
LANES = 128
SEL_ROWS = 16
SPLIT = 1
NEG = -1e37


def gate_kernel(dims, *refs):
    n_piece, n_key, heads, n_sel, n_cand, blocks, head_size = dims
    cand_s = refs[0]
    q_in = refs[1 : 1 + n_piece]
    k_in = refs[1 + n_piece : 1 + n_piece + n_key]
    refs = refs[1 + n_piece + n_key :]
    wq_in, wk_in = refs[:2]
    out_refs = refs[2 : 2 + n_piece]
    qbuf, kbuf, pool, qpool, teach, ms, ss, lv, sel_v, sel_s, wq_ref, wk_ref, sem_q, sem_k, sem_s, sem_w = refs[2 + n_piece :]
    stride = q_in[0].shape[0]
    span = stride - SEL_ROWS
    span_blocks = span // BLOCK
    n_slot = n_sel + 1
    rows = n_piece * heads * span_blocks
    exp_scale = math.log2(math.e) / math.sqrt(head_size)

    q_copies = [
        pltpu.make_async_copy(q_in[i], qbuf.at[pl.ds(i * stride, stride)], sem_q.at[i]) for i in range(n_piece)
    ]
    k_rows = k_in[0].shape[0]
    k_copies = [
        pltpu.make_async_copy(k_in[i], kbuf.at[pl.ds(i * k_rows, k_rows)], sem_k.at[i]) for i in range(n_key)
    ]
    w_copies = [
        pltpu.make_async_copy(wq_in, wq_ref, sem_w.at[0]),
        pltpu.make_async_copy(wk_in, wk_ref, sem_w.at[1]),
    ]
    for copy in q_copies + k_copies + w_copies:
        copy.start()
    for copy in q_copies:
        copy.wait()

    lane = lax.broadcasted_iota(jnp.int32, (1, LANES), 1)
    sub = lax.broadcasted_iota(jnp.int32, (8, 1), 0)
    listed = lane < heads * n_sel
    group = lax.broadcasted_iota(jnp.int32, (LANES, 1), 0) // n_sel + heads * n_sel == lane
    for i in range(n_piece):
        mine = qbuf[i * stride + span : (i + 1) * stride, :LANES].astype(jnp.float32)[:8].astype(jnp.int32)
        own = ((mine == sub) & listed).astype(jnp.float32).astype(jnp.bfloat16)
        own = jnp.dot(own, group.astype(jnp.float32).astype(jnp.bfloat16), preferred_element_type=jnp.float32)
        at = own.astype(jnp.int32)
        for m in range(n_cand):
            at = jnp.where((mine == m) & listed, cand_s[i * n_cand + m], at)
        sel_v[i] = at
        lv[i] = jnp.transpose(jnp.broadcast_to(at.astype(jnp.float32)[None], (LANES // 8, 8, LANES)).reshape(LANES, LANES)).astype(jnp.int32)
    sel_copy = pltpu.make_async_copy(sel_v, sel_s, sem_s)
    sel_copy.start()
    for copy in k_copies:
        copy.wait()

    def pool_step(i, carry):
        first = pl.multiple_of(i * 8 * BLOCK, 8 * BLOCK)
        keys = kbuf[pl.ds(first, 8 * BLOCK), :].astype(jnp.float32).reshape(8, BLOCK, head_size)
        at = pl.ds(pl.multiple_of(i * 8, 8), 8)
        pool[at, 0:head_size] = jnp.max(keys, axis=1)
        pool[at, head_size : 2 * head_size] = jnp.min(keys, axis=1)
        pool[at, 2 * head_size :] = jnp.sum(keys, axis=1) * (1.0 / BLOCK)
        return carry

    lax.fori_loop(0, blocks // 8, pool_step, 0)
    sel_copy.wait()

    low = lane < BLOCK
    zeros = jnp.zeros((BLOCK, head_size), jnp.bfloat16)
    pairs = span_blocks // 2

    def places(ph, t):
        piece = ph // heads
        head = ph - piece * heads
        at = [
            [sel_s[piece, 2 * t + half, head * n_sel + slot] for half in range(2)] for slot in range(n_sel)
        ]
        return at + [[cand_s[piece * n_cand + 2 * t + half] for half in range(2)]]

    def pair_step(ph, t):
        piece = ph // heads
        head = ph - piece * heads
        q_at = pl.ds(pl.multiple_of(piece * stride + t * 2 * BLOCK, SEL_ROWS), 2 * BLOCK)
        q = qbuf[q_at, pl.ds(pl.multiple_of(head * head_size, head_size), head_size)]
        q0, q1 = q[:BLOCK], q[BLOCK:]
        row = ph * span_blocks + 2 * t
        for half, x in enumerate((q0, q1)):
            qpool[pl.ds(row + half, 1), :] = jnp.sum(x.astype(jnp.float32), axis=0, keepdims=True) * (1.0 / BLOCK)
        rhs = jnp.concatenate(
            [jnp.concatenate([q0, zeros], axis=1), jnp.concatenate([zeros, q1], axis=1)], axis=0
        )
        lhs = jnp.concatenate(
            [
                jnp.concatenate(
                    [kbuf[pl.ds(pl.multiple_of(at * BLOCK, BLOCK), BLOCK), :] for at in both], axis=1
                )
                for both in places(ph, t)
            ],
            axis=0,
        )
        scores = lax.dot_general(lhs, rhs, (((1,), (1,)), ((), ())), preferred_element_type=jnp.float32)
        at = ph * pairs + t
        for slot in range(n_slot):
            part = scores[slot * BLOCK : (slot + 1) * BLOCK]
            top = jnp.max(part, axis=0, keepdims=True)
            ms[at, slot : slot + 1, :] = top
            ss[at, slot : slot + 1, :] = jnp.sum(jnp.exp2((part - top) * exp_scale), axis=0, keepdims=True)

    def head_step(ph, carry):
        for t in range(pairs):
            pair_step(ph, t)
        return carry


    slots = ms.shape[1]
    slot_row = lax.broadcasted_iota(jnp.int32, (slots, 1), 0)

    def combine(ph, t):
        piece = ph // heads
        head = ph - piece * heads
        row = ph * span_blocks + 2 * t
        at = ph * pairs + t
        drop = [sel_s[piece, 2 * t + half, heads * n_sel + head] for half in range(2)]
        keep = slot_row < jnp.where(low, n_slot - drop[0], n_slot - drop[1])
        tops = jnp.where(keep, ms[at], NEG)
        most = jnp.max(tops, axis=0, keepdims=True)
        weight = jnp.where(keep, jnp.exp2((tops - most) * exp_scale) * ss[at], 0.0)
        share = weight / jnp.sum(weight, axis=0, keepdims=True)
        for half in range(2):
            mine = low if half == 0 else jnp.logical_not(low)
            mean = jnp.sum(jnp.where(mine, share, 0.0), axis=1, keepdims=True) * (1.0 / BLOCK)
            column = lv[piece, pl.ds(pl.multiple_of(head * n_sel, n_sel), n_sel), 2 * t + half : 2 * t + half + 1]
            own = jnp.full((slots - n_sel, 1), cand_s[piece * n_cand + 2 * t + half], jnp.int32)
            column = jnp.concatenate([column, own], axis=0)
            for c in range(blocks // LANES):
                hit = column == lane + c * LANES
                teach[c, pl.ds(row + half, 1), :] = jnp.sum(
                    jnp.where(hit, mean, 0.0), axis=0, keepdims=True
                )

    def combine_step(ph, carry):
        for t in range(pairs):
            combine(ph, t)
        head_step(jnp.minimum(ph + 1, n_piece * heads - 1), 0)
        return carry

    head_step(0, 0)
    lax.fori_loop(0, n_piece * heads, combine_step, 0, unroll=4)

    for copy in w_copies:
        copy.wait()
    k_gate = jnp.dot(
        pool[...].astype(jnp.bfloat16), wk_ref[...], preferred_element_type=jnp.float32
    ).astype(jnp.bfloat16)
    q_gate = jnp.dot(
        qpool[...].astype(jnp.bfloat16), wq_ref[...], preferred_element_type=jnp.float32
    ).astype(jnp.bfloat16)
    logits = lax.dot_general(
        q_gate, k_gate, (((1,), (1,)), ((), ())), preferred_element_type=jnp.float32
    ) * (1.0 / math.sqrt(wq_ref.shape[1]))
    top = jnp.max(logits, axis=1, keepdims=True)
    log_gate = logits - top - jnp.log(jnp.sum(jnp.exp(logits - top), axis=1, keepdims=True))
    teacher = jnp.concatenate([teach[c] for c in range(blocks // LANES)], axis=1)
    positive = teacher > 0
    safe = jnp.where(positive, teacher, 1.0)
    kl = jnp.sum(jnp.where(positive, teacher * (jnp.log(safe) - log_gate), 0.0), axis=1, keepdims=True)
    r = lax.broadcasted_iota(jnp.int32, (rows, 1), 0)
    spread = jnp.where(r // span_blocks % heads + cand_s[n_piece * n_cand] == lane, kl, 0.0)
    r = lax.broadcasted_iota(jnp.int32, (1, rows), 1)
    b = lax.broadcasted_iota(jnp.int32, (8, 1), 0)
    for i in range(n_piece):
        pick = (r % span_blocks == b) & (r // (span_blocks * heads) == i) & (b < span_blocks)
        tile = jnp.dot(
            pick.astype(jnp.float32), spread, preferred_element_type=jnp.float32, precision=lax.Precision.HIGHEST
        )
        out_refs[i][...] = tile


def gate_call(cand, q_pieces, k_pieces, w_query, key_gate_weight, heads, n_sel, n_cand):
    head_size = w_query.shape[0]
    stride = q_pieces[0].shape[0]
    span_blocks = (stride - SEL_ROWS) // BLOCK
    n_piece = len(q_pieces)
    blocks = len(k_pieces) * k_pieces[0].shape[0] // BLOCK
    rows = n_piece * heads * span_blocks
    dims = (n_piece, len(k_pieces), heads, n_sel, n_cand, blocks, head_size)
    slots = -(-(n_sel + 1) // 8) * 8
    smem = pl.BlockSpec(memory_space=pltpu.SMEM)
    hbm = pl.BlockSpec(memory_space=pl.ANY)
    vmem = pl.BlockSpec(memory_space=pltpu.VMEM)
    return pl.pallas_call(
        functools.partial(gate_kernel, dims),
        out_shape=[jax.ShapeDtypeStruct((8, LANES), jnp.float32)] * n_piece,
        in_specs=[smem] + [hbm] * (n_piece + len(k_pieces) + 2),
        out_specs=[vmem] * n_piece,
        scratch_shapes=[
            pltpu.VMEM((n_piece * stride, heads * head_size), jnp.bfloat16),
            pltpu.VMEM((blocks * BLOCK, head_size), jnp.bfloat16),
            pltpu.VMEM((blocks, 3 * head_size), jnp.float32),
            pltpu.VMEM((rows, head_size), jnp.float32),
            pltpu.VMEM((blocks // LANES, rows, LANES), jnp.float32),
            pltpu.VMEM((rows // 2, slots, LANES), jnp.float32),
            pltpu.VMEM((rows // 2, slots, LANES), jnp.float32),
            pltpu.VMEM((n_piece, LANES, LANES), jnp.int32),
            pltpu.VMEM((n_piece, 8, LANES), jnp.int32),
            pltpu.SMEM((n_piece, 8, LANES), jnp.int32),
            pltpu.VMEM(w_query.shape, w_query.dtype),
            pltpu.VMEM(key_gate_weight.shape, key_gate_weight.dtype),
            pltpu.SemaphoreType.DMA((n_piece,)),
            pltpu.SemaphoreType.DMA((len(k_pieces),)),
            pltpu.SemaphoreType.DMA(()),
            pltpu.SemaphoreType.DMA((2,)),
        ],
        compiler_params=pltpu.CompilerParams(vmem_limit_bytes=40 * 1024 * 1024),
    )(cand, *q_pieces, *k_pieces, w_query, key_gate_weight)


def per_device(queries, key_state_rows, wanted, selected, w_query, key_gate_weight):
    n_ctx, n_pair = lax.axis_size("ctx"), lax.axis_size("pair")
    ctx, core = lax.axis_index("ctx"), lax.axis_index("pair")
    head_size = w_query.shape[0]
    span, key_width = key_state_rows.shape
    span_blocks = span // BLOCK
    q_heads = queries.shape[1] // head_size
    kv_heads = key_width // head_size
    heads = q_heads // kv_heads
    n_sel = selected.shape[2]
    plane = kv_heads if kv_heads in (1, 2, 4) and n_ctx % kv_heads == 0 and n_pair == 2 else 1
    layers = n_ctx // plane
    ring = plane > 1 and layers <= 4
    spot = ctx % plane
    layer = ctx // plane

    def place_of(block):
        if not ring:
            return block
        span_id = block // span_blocks
        other_ctx = span_id // n_pair
        step = (layer - other_ctx // plane) % layers
        which = (other_ctx % plane) ^ spot
        side = (span_id % n_pair) ^ core
        return ((side * layers + step) * plane + which) * span_blocks + block % span_blocks

    local_ids = jnp.arange(span_blocks, dtype=jnp.int32)
    candidates = []
    for p in range(plane if ring else 1):
        other_span = (ctx ^ p) * n_pair + core
        wants = lax.dynamic_index_in_dim(wanted, other_span, 0, keepdims=False)
        candidates.append(
            jnp.concatenate(
                [other_span * span_blocks + local_ids, (other_span ^ 1) * span_blocks + local_ids, wants]
            )
        )
    n_cand = candidates[0].shape[0]
    first_lane = spot * heads if ring else 0
    cand = jnp.concatenate(
        [place_of(jnp.concatenate(candidates)).astype(jnp.int32), jnp.full((1,), first_lane, jnp.int32)]
    )

    width = heads * head_size
    sel_rows = jnp.pad(
        selected.astype(jnp.bfloat16).reshape(span_blocks, kv_heads, heads * n_sel),
        ((0, SEL_ROWS - span_blocks), (0, 0), (0, width - heads * n_sel)),
    ).reshape(SEL_ROWS, q_heads * head_size)
    sent = jnp.concatenate([queries, sel_rows], axis=0)

    if not ring:
        gathered = lax.all_gather(key_state_rows, ("ctx", "pair"), axis=0, tiled=True)
        outs = []
        for g in range(kv_heads):
            (out,) = gate_call(
                cand,
                [sent[:, g * width : (g + 1) * width]],
                [gathered[:, g * head_size : (g + 1) * head_size]],
                w_query, key_gate_weight, heads, n_sel, n_cand,
            )
            outs.append(out[:span_blocks, :heads])
        return jnp.concatenate(outs, axis=1)

    def flipped(x, p):
        return x if p == 0 else lax.ppermute(x, "ctx", [(i, i ^ p) for i in range(n_ctx)])

    def other_core(x):
        return lax.ppermute(x, "pair", [(0, 1), (1, 0)])

    keys = [
        flipped(lax.dynamic_slice_in_dim(key_state_rows, (spot ^ p) * head_size, head_size, 1), p)
        for p in range(plane)
    ]
    parts = [lax.dynamic_slice_in_dim(sent, (spot ^ p) * width, width, 1) for p in range(plane)]
    per = plane // SPLIT
    streams = [[jnp.concatenate(keys[i * per : (i + 1) * per], axis=0)] for i in range(SPLIT)]
    heads_of, parts = lax.optimization_barrier(([x[0] for x in streams], parts))
    streams = [[x] for x in heads_of]
    pieces = [flipped(x, p) for p, x in enumerate(parts)]
    for i in range(layers - 1):
        if i == 2:
            tied = ([x[i] for x in streams], pieces[1:3], cand)
            heads_of, pieces[1:3], cand = lax.optimization_barrier(tied)
            for x, y in zip(streams, heads_of):
                x[i] = y
        for x in streams:
            x.append(lax.ppermute(x[i], "ctx", [(j, (j + plane) % n_ctx) for j in range(n_ctx)]))
    mine = [x[i] for i in range(layers) for x in streams]
    k_pieces = mine + [other_core(x) for x in mine]
    outs = gate_call(cand, pieces, k_pieces, w_query, key_gate_weight, heads, n_sel, n_cand)
    back = [flipped(x, p) for p, x in enumerate(outs)]
    return functools.reduce(jnp.add, back)[:span_blocks, :q_heads]


def solution(mesh):
    return jax.shard_map(
        per_device,
        mesh=mesh,
        in_specs=(
            P(("groups", "ctx", "pair"), "head"),
            P(("groups", "ctx", "pair"), "head"),
            P("groups", None),
            P(("groups", "ctx", "pair"), "head", None),
            P(),
            P(),
        ),
        out_specs=P(("groups", "ctx", "pair"), "head"),
        check_vma=False,
    )
```

```python
import functools
import math

import jax
import jax.numpy as jnp
from jax import lax
from jax.experimental import pallas as pl
from jax.experimental.pallas import tpu as pltpu
from jax.sharding import PartitionSpec as P

BLOCK = 64
LANES = 128
SEL_ROWS = 16
NEG = -1e37


def gate_kernel(dims, *refs):
    q_plan, n_piece, n_q, n_key, heads, n_sel, n_cand, blocks, head_size, stride = dims
    cand_s = refs[0]
    q_in = refs[1 : 1 + n_q]
    k_in = refs[1 + n_q : 1 + n_q + n_key]
    refs = refs[1 + n_q + n_key :]
    wq_in, wk_in = refs[:2]
    out_refs = refs[2 : 2 + n_piece]
    qbuf, kbuf, pool, qpool, teach, ms, ss, lv, sel_v, sel_s, wq_ref, wk_ref, sem_q, sem_k, sem_s, sem_w = refs[2 + n_piece :]
    span = stride - SEL_ROWS
    span_blocks = span // BLOCK
    n_slot = n_sel + 1
    rows = n_piece * heads * span_blocks
    exp_scale = math.log2(math.e) / math.sqrt(head_size)

    q_copies = [
        pltpu.make_async_copy(q_in[src].at[pl.ds(row, count)], qbuf.at[pl.ds(to, count)], sem_q.at[i])
        for i, (src, row, count, to) in enumerate(q_plan)
    ]
    k_copies, to = [], 0
    for i, k in enumerate(k_in):
        k_copies.append(pltpu.make_async_copy(k, kbuf.at[pl.ds(to, k.shape[0])], sem_k.at[i]))
        to += k.shape[0]
    w_copies = [
        pltpu.make_async_copy(wq_in, wq_ref, sem_w.at[0]),
        pltpu.make_async_copy(wk_in, wk_ref, sem_w.at[1]),
    ]
    for copy in q_copies + k_copies + w_copies:
        copy.start()
    for copy in q_copies:
        copy.wait()

    lane = lax.broadcasted_iota(jnp.int32, (1, LANES), 1)
    sub = lax.broadcasted_iota(jnp.int32, (8, 1), 0)
    listed = lane < heads * n_sel
    group = lax.broadcasted_iota(jnp.int32, (LANES, 1), 0) // n_sel + heads * n_sel == lane
    for i in range(n_piece):
        mine = qbuf[i * stride + span : (i + 1) * stride, :LANES].astype(jnp.float32)[:8].astype(jnp.int32)
        own = ((mine == sub) & listed).astype(jnp.float32).astype(jnp.bfloat16)
        own = jnp.dot(own, group.astype(jnp.float32).astype(jnp.bfloat16), preferred_element_type=jnp.float32)
        at = own.astype(jnp.int32)
        for m in range(n_cand):
            at = jnp.where((mine == m) & listed, cand_s[i * n_cand + m], at)
        sel_v[i] = at
        lv[i] = jnp.transpose(jnp.broadcast_to(at.astype(jnp.float32)[None], (LANES // 8, 8, LANES)).reshape(LANES, LANES)).astype(jnp.int32)
    sel_copy = pltpu.make_async_copy(sel_v, sel_s, sem_s)
    sel_copy.start()
    for copy in k_copies:
        copy.wait()

    def pool_step(i, carry):
        first = pl.multiple_of(i * 8 * BLOCK, 8 * BLOCK)
        keys = kbuf[pl.ds(first, 8 * BLOCK), :].astype(jnp.float32).reshape(8, BLOCK, head_size)
        at = pl.ds(pl.multiple_of(i * 8, 8), 8)
        pool[at, 0:head_size] = jnp.max(keys, axis=1)
        pool[at, head_size : 2 * head_size] = jnp.min(keys, axis=1)
        pool[at, 2 * head_size :] = jnp.sum(keys, axis=1) * (1.0 / BLOCK)
        return carry

    lax.fori_loop(0, blocks // 8, pool_step, 0)
    sel_copy.wait()

    low = lane < BLOCK
    zeros = jnp.zeros((BLOCK, head_size), jnp.bfloat16)
    pairs = span_blocks // 2

    def places(ph, t):
        piece = ph // heads
        head = ph - piece * heads
        at = [
            [sel_s[piece, 2 * t + half, head * n_sel + slot] for half in range(2)] for slot in range(n_sel)
        ]
        return at + [[cand_s[piece * n_cand + 2 * t + half] for half in range(2)]]

    def pair_step(ph, t):
        piece = ph // heads
        head = ph - piece * heads
        q_at = pl.ds(pl.multiple_of(piece * stride + t * 2 * BLOCK, SEL_ROWS), 2 * BLOCK)
        q = qbuf[q_at, pl.ds(pl.multiple_of(head * head_size, head_size), head_size)]
        q0, q1 = q[:BLOCK], q[BLOCK:]
        row = ph * span_blocks + 2 * t
        for half, x in enumerate((q0, q1)):
            qpool[pl.ds(row + half, 1), :] = jnp.sum(x.astype(jnp.float32), axis=0, keepdims=True) * (1.0 / BLOCK)
        rhs = jnp.concatenate(
            [jnp.concatenate([q0, zeros], axis=1), jnp.concatenate([zeros, q1], axis=1)], axis=0
        )
        lhs = jnp.concatenate(
            [
                jnp.concatenate(
                    [kbuf[pl.ds(pl.multiple_of(at * BLOCK, BLOCK), BLOCK), :] for at in both], axis=1
                )
                for both in places(ph, t)
            ],
            axis=0,
        )
        scores = lax.dot_general(lhs, rhs, (((1,), (1,)), ((), ())), preferred_element_type=jnp.float32)
        at = ph * pairs + t
        for slot in range(n_slot):
            part = scores[slot * BLOCK : (slot + 1) * BLOCK]
            top = jnp.max(part, axis=0, keepdims=True)
            ms[at, slot : slot + 1, :] = top
            ss[at, slot : slot + 1, :] = jnp.sum(jnp.exp2((part - top) * exp_scale), axis=0, keepdims=True)

    def head_step(ph, carry):
        for t in range(pairs):
            pair_step(ph, t)
        return carry


    slots = ms.shape[1]
    slot_row = lax.broadcasted_iota(jnp.int32, (slots, 1), 0)

    def combine(ph, t):
        piece = ph // heads
        head = ph - piece * heads
        row = ph * span_blocks + 2 * t
        at = ph * pairs + t
        drop = [sel_s[piece, 2 * t + half, heads * n_sel + head] for half in range(2)]
        keep = slot_row < jnp.where(low, n_slot - drop[0], n_slot - drop[1])
        tops = jnp.where(keep, ms[at], NEG)
        most = jnp.max(tops, axis=0, keepdims=True)
        weight = jnp.where(keep, jnp.exp2((tops - most) * exp_scale) * ss[at], 0.0)
        share = weight / jnp.sum(weight, axis=0, keepdims=True)
        for half in range(2):
            mine = low if half == 0 else jnp.logical_not(low)
            mean = jnp.sum(jnp.where(mine, share, 0.0), axis=1, keepdims=True) * (1.0 / BLOCK)
            column = lv[piece, pl.ds(pl.multiple_of(head * n_sel, n_sel), n_sel), 2 * t + half : 2 * t + half + 1]
            own = jnp.full((slots - n_sel, 1), cand_s[piece * n_cand + 2 * t + half], jnp.int32)
            column = jnp.concatenate([column, own], axis=0)
            for c in range(blocks // LANES):
                hit = column == lane + c * LANES
                teach[c, pl.ds(row + half, 1), :] = jnp.sum(
                    jnp.where(hit, mean, 0.0), axis=0, keepdims=True
                )

    def combine_step(ph, carry):
        for t in range(pairs):
            combine(ph, t)
        head_step(jnp.minimum(ph + 1, n_piece * heads - 1), 0)
        return carry

    head_step(0, 0)
    lax.fori_loop(0, n_piece * heads, combine_step, 0, unroll=7)

    for copy in w_copies:
        copy.wait()
    k_gate = jnp.dot(
        pool[...].astype(jnp.bfloat16), wk_ref[...], preferred_element_type=jnp.float32
    ).astype(jnp.bfloat16)
    q_gate = jnp.dot(
        qpool[...].astype(jnp.bfloat16), wq_ref[...], preferred_element_type=jnp.float32
    ).astype(jnp.bfloat16)
    logits = lax.dot_general(
        q_gate, k_gate, (((1,), (1,)), ((), ())), preferred_element_type=jnp.float32
    ) * (1.0 / math.sqrt(wq_ref.shape[1]))
    top = jnp.max(logits, axis=1, keepdims=True)
    log_gate = logits - top - jnp.log(jnp.sum(jnp.exp(logits - top), axis=1, keepdims=True))
    teacher = jnp.concatenate([teach[c] for c in range(blocks // LANES)], axis=1)
    positive = teacher > 0
    safe = jnp.where(positive, teacher, 1.0)
    kl = jnp.sum(jnp.where(positive, teacher * (jnp.log(safe) - log_gate), 0.0), axis=1, keepdims=True)
    r = lax.broadcasted_iota(jnp.int32, (rows, 1), 0)
    spread = jnp.where(r // span_blocks % heads + cand_s[n_piece * n_cand] == lane, kl, 0.0)
    r = lax.broadcasted_iota(jnp.int32, (1, rows), 1)
    b = lax.broadcasted_iota(jnp.int32, (8 * n_piece, 1), 0)
    pick = (r % span_blocks == b % 8) & (r // (span_blocks * heads) == b // 8)
    tiles = jnp.dot(
        pick.astype(jnp.float32), spread, preferred_element_type=jnp.float32, precision=lax.Precision.HIGHEST
    )
    for i in range(n_piece):
        out_refs[i][...] = tiles[8 * i : 8 * i + 8]


def gate_call(cand, q_plan, q_pieces, k_pieces, w_query, key_gate_weight, stride, heads, n_sel, n_cand):
    head_size = w_query.shape[0]
    span_blocks = (stride - SEL_ROWS) // BLOCK
    n_piece = sum(count for _, _, count, _ in q_plan) // stride
    blocks = sum(x.shape[0] for x in k_pieces) // BLOCK
    rows = n_piece * heads * span_blocks
    dims = (
        tuple(q_plan), n_piece, len(q_pieces), len(k_pieces), heads, n_sel, n_cand, blocks, head_size, stride,
    )
    slots = -(-(n_sel + 1) // 8) * 8
    smem = pl.BlockSpec(memory_space=pltpu.SMEM)
    hbm = pl.BlockSpec(memory_space=pl.ANY)
    vmem = pl.BlockSpec(memory_space=pltpu.VMEM)
    return pl.pallas_call(
        functools.partial(gate_kernel, dims),
        out_shape=[jax.ShapeDtypeStruct((8, LANES), jnp.float32)] * n_piece,
        in_specs=[smem] + [hbm] * (len(q_pieces) + len(k_pieces) + 2),
        out_specs=[vmem] * n_piece,
        scratch_shapes=[
            pltpu.VMEM((n_piece * stride, heads * head_size), jnp.bfloat16),
            pltpu.VMEM((blocks * BLOCK, head_size), jnp.bfloat16),
            pltpu.VMEM((blocks, 3 * head_size), jnp.float32),
            pltpu.VMEM((rows, head_size), jnp.float32),
            pltpu.VMEM((blocks // LANES, rows, LANES), jnp.float32),
            pltpu.VMEM((rows // 2, slots, LANES), jnp.float32),
            pltpu.VMEM((rows // 2, slots, LANES), jnp.float32),
            pltpu.VMEM((n_piece, LANES, LANES), jnp.int32),
            pltpu.VMEM((n_piece, 8, LANES), jnp.int32),
            pltpu.SMEM((n_piece, 8, LANES), jnp.int32),
            pltpu.VMEM(w_query.shape, w_query.dtype),
            pltpu.VMEM(key_gate_weight.shape, key_gate_weight.dtype),
            pltpu.SemaphoreType.DMA((len(q_plan),)),
            pltpu.SemaphoreType.DMA((len(k_pieces),)),
            pltpu.SemaphoreType.DMA(()),
            pltpu.SemaphoreType.DMA((2,)),
        ],
        compiler_params=pltpu.CompilerParams(vmem_limit_bytes=40 * 1024 * 1024),
    )(cand, *q_pieces, *k_pieces, w_query, key_gate_weight)


def per_device(queries, key_state_rows, wanted, selected, w_query, key_gate_weight):
    n_ctx, n_pair = lax.axis_size("ctx"), lax.axis_size("pair")
    ctx, core = lax.axis_index("ctx"), lax.axis_index("pair")
    head_size = w_query.shape[0]
    span, key_width = key_state_rows.shape
    span_blocks = span // BLOCK
    q_heads = queries.shape[1] // head_size
    kv_heads = key_width // head_size
    heads = q_heads // kv_heads
    n_sel = selected.shape[2]
    plane = kv_heads if kv_heads in (1, 2, 4) and n_ctx % kv_heads == 0 and n_pair == 2 else 1
    layers = n_ctx // plane
    ring = plane > 1 and layers <= 4
    spot = ctx % plane
    layer = ctx // plane

    def place_of(block):
        if not ring:
            return block
        span_id = block // span_blocks
        other_ctx = span_id // n_pair
        step = (layer - other_ctx // plane) % layers
        which = (other_ctx % plane) ^ spot
        side = (span_id % n_pair) ^ core
        last = layers - 1
        at = jnp.where(step == last, last * n_pair + side, side * last + step)
        return (at * plane + which) * span_blocks + block % span_blocks

    local_ids = jnp.arange(span_blocks, dtype=jnp.int32)
    candidates = []
    for p in range(plane if ring else 1):
        other_span = (ctx ^ p) * n_pair + core
        wants = lax.dynamic_index_in_dim(wanted, other_span, 0, keepdims=False)
        candidates.append(
            jnp.concatenate(
                [other_span * span_blocks + local_ids, (other_span ^ 1) * span_blocks + local_ids, wants]
            )
        )
    n_cand = candidates[0].shape[0]
    first_lane = spot * heads if ring else 0
    cand = jnp.concatenate(
        [place_of(jnp.concatenate(candidates)).astype(jnp.int32), jnp.full((1,), first_lane, jnp.int32)]
    )

    width = heads * head_size
    stride = span + SEL_ROWS
    sel_rows = jnp.pad(
        selected.astype(jnp.bfloat16).reshape(span_blocks, kv_heads, heads * n_sel),
        ((0, SEL_ROWS - span_blocks), (0, 0), (0, width - heads * n_sel)),
    ).reshape(SEL_ROWS, q_heads * head_size)
    sent = jnp.concatenate([queries, sel_rows], axis=0)
    if not ring:
        gathered = lax.all_gather(key_state_rows, ("ctx", "pair"), axis=0, tiled=True)
        outs = []
        for g in range(kv_heads):
            (out,) = gate_call(
                cand,
                [(0, 0, stride, 0)],
                [sent[:, g * width : (g + 1) * width]],
                [gathered[:, g * head_size : (g + 1) * head_size]],
                w_query, key_gate_weight, stride, heads, n_sel, n_cand,
            )
            outs.append(out[:span_blocks, :heads])
        return jnp.concatenate(outs, axis=1)

    def flipped(x, p):
        return x if p == 0 else lax.ppermute(x, "ctx", [(i, i ^ p) for i in range(n_ctx)])

    def other_core(x):
        return lax.ppermute(x, "pair", [(0, 1), (1, 0)])

    keys = [
        flipped(lax.dynamic_slice_in_dim(key_state_rows, (spot ^ p) * head_size, head_size, 1), p)
        for p in range(plane)
    ]
    parts = [lax.dynamic_slice_in_dim(sent, (spot ^ p) * width, width, 1) for p in range(plane)]
    steps = [jnp.concatenate(keys, axis=0)]
    other = []
    steps[0], parts = lax.optimization_barrier((steps[0], parts))
    pieces = [flipped(x, p) for p, x in enumerate(parts)]
    for i in range(layers - 1):
        if i == 2:
            steps[2], pieces[1:3], cand = lax.optimization_barrier((steps[2], pieces[1:3], cand))
        steps.append(lax.ppermute(steps[i], "ctx", [(j, (j + plane) % n_ctx) for j in range(n_ctx)]))
    other += [other_core(x) for x in steps[len(other) :]]
    k_pieces = [jnp.concatenate(steps[:-1] + other[:-1], axis=0), steps[-1], other[-1]]
    q_pieces = pieces
    q_plan, to = [], 0
    for i, x in enumerate(q_pieces):
        q_plan.append((i, 0, x.shape[0], to))
        to += x.shape[0]
    outs = gate_call(
        cand, q_plan, q_pieces, k_pieces, w_query, key_gate_weight, stride, heads, n_sel, n_cand
    )
    back = [flipped(x, p) for p, x in enumerate(outs)]
    return functools.reduce(jnp.add, back)[:span_blocks, :q_heads]


def solution(mesh):
    return jax.shard_map(
        per_device,
        mesh=mesh,
        in_specs=(
            P(("groups", "ctx", "pair"), "head"),
            P(("groups", "ctx", "pair"), "head"),
            P("groups", None),
            P(("groups", "ctx", "pair"), "head", None),
            P(),
            P(),
        ),
        out_specs=P(("groups", "ctx", "pair"), "head"),
        check_vma=False,
    )
```

```python
import functools
import math

import jax
import jax.numpy as jnp
from jax import lax
from jax.experimental import pallas as pl
from jax.experimental.pallas import tpu as pltpu
from jax.sharding import PartitionSpec as P

BLOCK = 64
LANES = 128
SEL_ROWS = 16
NEG = -1e37


def gate_kernel(dims, *refs):
    q_plan, n_piece, n_q, n_key, heads, n_sel, n_cand, blocks, head_size, stride = dims
    cand_s = refs[0]
    q_in = refs[1 : 1 + n_q]
    k_in = refs[1 + n_q : 1 + n_q + n_key]
    refs = refs[1 + n_q + n_key :]
    wq_in, wk_in = refs[:2]
    out_refs = refs[2 : 2 + n_piece]
    qbuf, kbuf, pool, qpool, teach, ms, ss, lv, sel_v, sel_s, wq_ref, wk_ref, sem_q, sem_k, sem_s, sem_w = refs[2 + n_piece :]
    span = stride - SEL_ROWS
    span_blocks = span // BLOCK
    n_slot = n_sel + 1
    rows = n_piece * heads * span_blocks
    exp_scale = math.log2(math.e) / math.sqrt(head_size)

    q_copies = [
        pltpu.make_async_copy(q_in[src].at[pl.ds(row, count)], qbuf.at[pl.ds(to, count)], sem_q.at[i])
        for i, (src, row, count, to) in enumerate(q_plan)
    ]
    k_copies, to = [], 0
    for i, k in enumerate(k_in):
        k_copies.append(pltpu.make_async_copy(k, kbuf.at[pl.ds(to, k.shape[0])], sem_k.at[i]))
        to += k.shape[0]
    w_copies = [
        pltpu.make_async_copy(wq_in, wq_ref, sem_w.at[0]),
        pltpu.make_async_copy(wk_in, wk_ref, sem_w.at[1]),
    ]
    for copy in q_copies + k_copies + w_copies:
        copy.start()
    for copy in q_copies:
        copy.wait()

    lane = lax.broadcasted_iota(jnp.int32, (1, LANES), 1)
    sub = lax.broadcasted_iota(jnp.int32, (8, 1), 0)
    listed = lane < heads * n_sel
    group = lax.broadcasted_iota(jnp.int32, (LANES, 1), 0) // n_sel + heads * n_sel == lane
    for i in range(n_piece):
        mine = qbuf[i * stride + span : (i + 1) * stride, :LANES].astype(jnp.float32)[:8].astype(jnp.int32)
        own = ((mine == sub) & listed).astype(jnp.float32).astype(jnp.bfloat16)
        own = jnp.dot(own, group.astype(jnp.float32).astype(jnp.bfloat16), preferred_element_type=jnp.float32)
        at = own.astype(jnp.int32)
        for m in range(n_cand):
            at = jnp.where((mine == m) & listed, cand_s[i * n_cand + m], at)
        sel_v[i] = at
        lv[i] = jnp.transpose(jnp.broadcast_to(at.astype(jnp.float32)[None], (LANES // 8, 8, LANES)).reshape(LANES, LANES)).astype(jnp.int32)
    sel_copy = pltpu.make_async_copy(sel_v, sel_s, sem_s)
    sel_copy.start()
    for copy in k_copies:
        copy.wait()

    def pool_step(i, carry):
        first = pl.multiple_of(i * 8 * BLOCK, 8 * BLOCK)
        keys = kbuf[pl.ds(first, 8 * BLOCK), :].astype(jnp.float32).reshape(8, BLOCK, head_size)
        at = pl.ds(pl.multiple_of(i * 8, 8), 8)
        pool[at, 0:head_size] = jnp.max(keys, axis=1)
        pool[at, head_size : 2 * head_size] = jnp.min(keys, axis=1)
        pool[at, 2 * head_size :] = jnp.sum(keys, axis=1) * (1.0 / BLOCK)
        return carry

    lax.fori_loop(0, blocks // 8, pool_step, 0)
    sel_copy.wait()

    low = lane < BLOCK
    zeros = jnp.zeros((BLOCK, head_size), jnp.bfloat16)
    pairs = span_blocks // 2

    def places(ph, t):
        piece = ph // heads
        head = ph - piece * heads
        at = [
            [sel_s[piece, 2 * t + half, head * n_sel + slot] for half in range(2)] for slot in range(n_sel)
        ]
        return at + [[cand_s[piece * n_cand + 2 * t + half] for half in range(2)]]

    def pair_step(ph, t):
        piece = ph // heads
        head = ph - piece * heads
        q_at = pl.ds(pl.multiple_of(piece * stride + t * 2 * BLOCK, SEL_ROWS), 2 * BLOCK)
        q = qbuf[q_at, pl.ds(pl.multiple_of(head * head_size, head_size), head_size)]
        q0, q1 = q[:BLOCK], q[BLOCK:]
        row = ph * span_blocks + 2 * t
        for half, x in enumerate((q0, q1)):
            qpool[pl.ds(row + half, 1), :] = jnp.sum(x.astype(jnp.float32), axis=0, keepdims=True) * (1.0 / BLOCK)
        rhs = jnp.concatenate(
            [jnp.concatenate([q0, zeros], axis=1), jnp.concatenate([zeros, q1], axis=1)], axis=0
        )
        lhs = jnp.concatenate(
            [
                jnp.concatenate(
                    [kbuf[pl.ds(pl.multiple_of(at * BLOCK, BLOCK), BLOCK), :] for at in both], axis=1
                )
                for both in places(ph, t)
            ],
            axis=0,
        )
        scores = lax.dot_general(lhs, rhs, (((1,), (1,)), ((), ())), preferred_element_type=jnp.float32)
        at = ph * pairs + t
        for slot in range(n_slot):
            part = scores[slot * BLOCK : (slot + 1) * BLOCK]
            top = jnp.max(part, axis=0, keepdims=True)
            ms[at, slot : slot + 1, :] = top
            ss[at, slot : slot + 1, :] = jnp.sum(jnp.exp2((part - top) * exp_scale), axis=0, keepdims=True)

    def head_step(ph, carry):
        for t in range(pairs):
            pair_step(ph, t)
        return carry


    slots = ms.shape[1]
    slot_row = lax.broadcasted_iota(jnp.int32, (slots, 1), 0)

    def combine(ph, t):
        piece = ph // heads
        head = ph - piece * heads
        row = ph * span_blocks + 2 * t
        at = ph * pairs + t
        drop = [sel_s[piece, 2 * t + half, heads * n_sel + head] for half in range(2)]
        keep = slot_row < jnp.where(low, n_slot - drop[0], n_slot - drop[1])
        tops = jnp.where(keep, ms[at], NEG)
        most = jnp.max(tops, axis=0, keepdims=True)
        weight = jnp.where(keep, jnp.exp2((tops - most) * exp_scale) * ss[at], 0.0)
        share = weight / jnp.sum(weight, axis=0, keepdims=True)
        for half in range(2):
            mine = low if half == 0 else jnp.logical_not(low)
            mean = jnp.sum(jnp.where(mine, share, 0.0), axis=1, keepdims=True) * (1.0 / BLOCK)
            column = lv[piece, pl.ds(pl.multiple_of(head * n_sel, n_sel), n_sel), 2 * t + half : 2 * t + half + 1]
            own = jnp.full((slots - n_sel, 1), cand_s[piece * n_cand + 2 * t + half], jnp.int32)
            column = jnp.concatenate([column, own], axis=0)
            for c in range(blocks // LANES):
                hit = column == lane + c * LANES
                teach[c, pl.ds(row + half, 1), :] = jnp.sum(
                    jnp.where(hit, mean, 0.0), axis=0, keepdims=True
                )

    def combine_step(ph, carry):
        for t in range(pairs):
            combine(ph, t)
        head_step(jnp.minimum(ph + 1, n_piece * heads - 1), 0)
        return carry

    head_step(0, 0)
    lax.fori_loop(0, n_piece * heads, combine_step, 0, unroll=14)

    for copy in w_copies:
        copy.wait()
    k_gate = jnp.dot(
        pool[...].astype(jnp.bfloat16), wk_ref[...], preferred_element_type=jnp.float32
    ).astype(jnp.bfloat16)
    q_gate = jnp.dot(
        qpool[...].astype(jnp.bfloat16), wq_ref[...], preferred_element_type=jnp.float32
    ).astype(jnp.bfloat16)
    logits = lax.dot_general(
        q_gate, k_gate, (((1,), (1,)), ((), ())), preferred_element_type=jnp.float32
    ) * (1.0 / math.sqrt(wq_ref.shape[1]))
    top = jnp.max(logits, axis=1, keepdims=True)
    log_gate = logits - top - jnp.log(jnp.sum(jnp.exp(logits - top), axis=1, keepdims=True))
    teacher = jnp.concatenate([teach[c] for c in range(blocks // LANES)], axis=1)
    positive = teacher > 0
    safe = jnp.where(positive, teacher, 1.0)
    kl = jnp.sum(jnp.where(positive, teacher * (jnp.log(safe) - log_gate), 0.0), axis=1, keepdims=True)
    r = lax.broadcasted_iota(jnp.int32, (rows, 1), 0)
    spread = jnp.where(r // span_blocks % heads + cand_s[n_piece * n_cand] == lane, kl, 0.0)
    r = lax.broadcasted_iota(jnp.int32, (1, rows), 1)
    b = lax.broadcasted_iota(jnp.int32, (8 * n_piece, 1), 0)
    pick = (r % span_blocks == b % 8) & (r // (span_blocks * heads) == b // 8)
    tiles = jnp.dot(
        pick.astype(jnp.float32), spread, preferred_element_type=jnp.float32, precision=lax.Precision.HIGHEST
    )
    for i in range(n_piece):
        out_refs[i][...] = tiles[8 * i : 8 * i + 8]


def gate_call(cand, q_plan, q_pieces, k_pieces, w_query, key_gate_weight, stride, heads, n_sel, n_cand):
    head_size = w_query.shape[0]
    span_blocks = (stride - SEL_ROWS) // BLOCK
    n_piece = sum(count for _, _, count, _ in q_plan) // stride
    blocks = sum(x.shape[0] for x in k_pieces) // BLOCK
    rows = n_piece * heads * span_blocks
    dims = (
        tuple(q_plan), n_piece, len(q_pieces), len(k_pieces), heads, n_sel, n_cand, blocks, head_size, stride,
    )
    slots = -(-(n_sel + 1) // 8) * 8
    smem = pl.BlockSpec(memory_space=pltpu.SMEM)
    hbm = pl.BlockSpec(memory_space=pl.ANY)
    vmem = pl.BlockSpec(memory_space=pltpu.VMEM)
    return pl.pallas_call(
        functools.partial(gate_kernel, dims),
        out_shape=[jax.ShapeDtypeStruct((8, LANES), jnp.float32)] * n_piece,
        in_specs=[smem] + [hbm] * (len(q_pieces) + len(k_pieces) + 2),
        out_specs=[vmem] * n_piece,
        scratch_shapes=[
            pltpu.VMEM((n_piece * stride, heads * head_size), jnp.bfloat16),
            pltpu.VMEM((blocks * BLOCK, head_size), jnp.bfloat16),
            pltpu.VMEM((blocks, 3 * head_size), jnp.float32),
            pltpu.VMEM((rows, head_size), jnp.float32),
            pltpu.VMEM((blocks // LANES, rows, LANES), jnp.float32),
            pltpu.VMEM((rows // 2, slots, LANES), jnp.float32),
            pltpu.VMEM((rows // 2, slots, LANES), jnp.float32),
            pltpu.VMEM((n_piece, LANES, LANES), jnp.int32),
            pltpu.VMEM((n_piece, 8, LANES), jnp.int32),
            pltpu.SMEM((n_piece, 8, LANES), jnp.int32),
            pltpu.VMEM(w_query.shape, w_query.dtype),
            pltpu.VMEM(key_gate_weight.shape, key_gate_weight.dtype),
            pltpu.SemaphoreType.DMA((len(q_plan),)),
            pltpu.SemaphoreType.DMA((len(k_pieces),)),
            pltpu.SemaphoreType.DMA(()),
            pltpu.SemaphoreType.DMA((2,)),
        ],
        compiler_params=pltpu.CompilerParams(vmem_limit_bytes=40 * 1024 * 1024),
    )(cand, *q_pieces, *k_pieces, w_query, key_gate_weight)


def per_device(queries, key_state_rows, wanted, selected, w_query, key_gate_weight):
    n_ctx, n_pair = lax.axis_size("ctx"), lax.axis_size("pair")
    ctx, core = lax.axis_index("ctx"), lax.axis_index("pair")
    head_size = w_query.shape[0]
    span, key_width = key_state_rows.shape
    span_blocks = span // BLOCK
    q_heads = queries.shape[1] // head_size
    kv_heads = key_width // head_size
    heads = q_heads // kv_heads
    n_sel = selected.shape[2]
    plane = kv_heads if kv_heads in (1, 2, 4) and n_ctx % kv_heads == 0 and n_pair == 2 else 1
    layers = n_ctx // plane
    ring = plane > 1 and layers <= 4
    spot = ctx % plane
    layer = ctx // plane

    def place_of(block):
        if not ring:
            return block
        span_id = block // span_blocks
        other_ctx = span_id // n_pair
        step = (layer - other_ctx // plane) % layers
        which = (other_ctx % plane) ^ spot
        side = (span_id % n_pair) ^ core
        last = layers - 1
        at = jnp.where(step == last, last * n_pair + side, side * last + step)
        return (at * plane + which) * span_blocks + block % span_blocks

    local_ids = jnp.arange(span_blocks, dtype=jnp.int32)
    candidates = []
    for p in range(plane if ring else 1):
        other_span = (ctx ^ p) * n_pair + core
        wants = lax.dynamic_index_in_dim(wanted, other_span, 0, keepdims=False)
        candidates.append(
            jnp.concatenate(
                [other_span * span_blocks + local_ids, (other_span ^ 1) * span_blocks + local_ids, wants]
            )
        )
    n_cand = candidates[0].shape[0]
    first_lane = spot * heads if ring else 0
    cand = jnp.concatenate(
        [place_of(jnp.concatenate(candidates)).astype(jnp.int32), jnp.full((1,), first_lane, jnp.int32)]
    )

    width = heads * head_size
    stride = span + SEL_ROWS
    sel_rows = jnp.pad(
        selected.astype(jnp.bfloat16).reshape(span_blocks, kv_heads, heads * n_sel),
        ((0, SEL_ROWS - span_blocks), (0, 0), (0, width - heads * n_sel)),
    ).reshape(SEL_ROWS, q_heads * head_size)
    sent = jnp.concatenate([queries, sel_rows], axis=0)
    if not ring:
        gathered = lax.all_gather(key_state_rows, ("ctx", "pair"), axis=0, tiled=True)
        outs = []
        for g in range(kv_heads):
            (out,) = gate_call(
                cand,
                [(0, 0, stride, 0)],
                [sent[:, g * width : (g + 1) * width]],
                [gathered[:, g * head_size : (g + 1) * head_size]],
                w_query, key_gate_weight, stride, heads, n_sel, n_cand,
            )
            outs.append(out[:span_blocks, :heads])
        return jnp.concatenate(outs, axis=1)

    def flipped(x, p):
        return x if p == 0 else lax.ppermute(x, "ctx", [(i, i ^ p) for i in range(n_ctx)])

    def other_core(x):
        return lax.ppermute(x, "pair", [(0, 1), (1, 0)])

    keys = [
        flipped(lax.dynamic_slice_in_dim(key_state_rows, (spot ^ p) * head_size, head_size, 1), p)
        for p in range(plane)
    ]
    parts = [lax.dynamic_slice_in_dim(sent, (spot ^ p) * width, width, 1) for p in range(plane)]
    steps = [jnp.concatenate(keys, axis=0)]
    other = []
    steps[0], parts = lax.optimization_barrier((steps[0], parts))
    pieces = [flipped(x, p) for p, x in enumerate(parts)]
    for i in range(layers - 1):
        if i == 2:
            steps[2], pieces[1:3], cand = lax.optimization_barrier((steps[2], pieces[1:3], cand))
        steps.append(lax.ppermute(steps[i], "ctx", [(j, (j + plane) % n_ctx) for j in range(n_ctx)]))
    other += [other_core(x) for x in steps[len(other) :]]
    k_pieces = [jnp.concatenate(steps[:-1] + other[:-1], axis=0), steps[-1], other[-1]]
    q_pieces = pieces
    q_plan, to = [], 0
    for i, x in enumerate(q_pieces):
        q_plan.append((i, 0, x.shape[0], to))
        to += x.shape[0]
    outs = gate_call(
        cand, q_plan, q_pieces, k_pieces, w_query, key_gate_weight, stride, heads, n_sel, n_cand
    )
    back = [flipped(x, p) for p, x in enumerate(outs)]
    return functools.reduce(jnp.add, [x[:span_blocks, :q_heads] for x in back])


def solution(mesh):
    return jax.shard_map(
        per_device,
        mesh=mesh,
        in_specs=(
            P(("groups", "ctx", "pair"), "head"),
            P(("groups", "ctx", "pair"), "head"),
            P("groups", None),
            P(("groups", "ctx", "pair"), "head", None),
            P(),
            P(),
        ),
        out_specs=P(("groups", "ctx", "pair"), "head"),
        check_vma=False,
    )
```

```python
import functools
import math

import jax
import jax.numpy as jnp
from jax import lax
from jax.experimental import pallas as pl
from jax.experimental.pallas import tpu as pltpu
from jax.sharding import PartitionSpec as P

BLOCK = 64
LANES = 128
SEL_ROWS = 16
NEG = -1e37


def gate_kernel(dims, *refs):
    q_plan, n_piece, n_q, n_key, heads, n_sel, n_cand, blocks, head_size, stride = dims
    cand_s = refs[0]
    q_in = refs[1 : 1 + n_q]
    k_in = refs[1 + n_q : 1 + n_q + n_key]
    refs = refs[1 + n_q + n_key :]
    wq_in, wk_in = refs[:2]
    out_refs = refs[2 : 2 + n_piece]
    qbuf, kbuf, pool, qpool, teach, ms, ss, lv, sel_v, sel_s, wq_ref, wk_ref, sem_q, sem_k, sem_s, sem_w = refs[2 + n_piece :]
    span = stride - SEL_ROWS
    span_blocks = span // BLOCK
    n_slot = n_sel + 1
    rows = n_piece * heads * span_blocks
    exp_scale = math.log2(math.e) / math.sqrt(head_size)

    q_copies = [
        pltpu.make_async_copy(q_in[src].at[pl.ds(row, count)], qbuf.at[pl.ds(to, count)], sem_q.at[i])
        for i, (src, row, count, to) in enumerate(q_plan)
    ]
    k_copies, to = [], 0
    for i, k in enumerate(k_in):
        k_copies.append(pltpu.make_async_copy(k, kbuf.at[pl.ds(to, k.shape[0])], sem_k.at[i]))
        to += k.shape[0]
    w_copies = [
        pltpu.make_async_copy(wq_in, wq_ref, sem_w.at[0]),
        pltpu.make_async_copy(wk_in, wk_ref, sem_w.at[1]),
    ]
    for copy in q_copies + k_copies + w_copies:
        copy.start()
    for copy in q_copies:
        copy.wait()

    lane = lax.broadcasted_iota(jnp.int32, (1, LANES), 1)
    sub = lax.broadcasted_iota(jnp.int32, (8, 1), 0)
    listed = lane < heads * n_sel
    group = lax.broadcasted_iota(jnp.int32, (LANES, 1), 0) // n_sel + heads * n_sel == lane
    for i in range(n_piece):
        mine = qbuf[i * stride + span : (i + 1) * stride, :LANES].astype(jnp.float32)[:8].astype(jnp.int32)
        own = ((mine == sub) & listed).astype(jnp.float32).astype(jnp.bfloat16)
        own = jnp.dot(own, group.astype(jnp.float32).astype(jnp.bfloat16), preferred_element_type=jnp.float32)
        at = own.astype(jnp.int32)
        for m in range(n_cand):
            at = jnp.where((mine == m) & listed, cand_s[i * n_cand + m], at)
        sel_v[i] = at
        lv[i] = jnp.transpose(jnp.broadcast_to(at.astype(jnp.float32)[None], (LANES // 8, 8, LANES)).reshape(LANES, LANES)).astype(jnp.int32)
    sel_copy = pltpu.make_async_copy(sel_v, sel_s, sem_s)
    sel_copy.start()
    for copy in k_copies:
        copy.wait()

    def pool_step(i, carry):
        first = pl.multiple_of(i * 8 * BLOCK, 8 * BLOCK)
        keys = kbuf[pl.ds(first, 8 * BLOCK), :].astype(jnp.float32).reshape(8, BLOCK, head_size)
        at = pl.ds(pl.multiple_of(i * 8, 8), 8)
        pool[at, 0:head_size] = jnp.max(keys, axis=1)
        pool[at, head_size : 2 * head_size] = jnp.min(keys, axis=1)
        pool[at, 2 * head_size :] = jnp.sum(keys, axis=1) * (1.0 / BLOCK)
        return carry

    lax.fori_loop(0, blocks // 8, pool_step, 0)
    sel_copy.wait()

    low = lane < BLOCK
    zeros = jnp.zeros((BLOCK, head_size), jnp.bfloat16)
    pairs = span_blocks // 2

    def places(ph, t):
        piece = ph // heads
        head = ph - piece * heads
        at = [
            [sel_s[piece, 2 * t + half, head * n_sel + slot] for half in range(2)] for slot in range(n_sel)
        ]
        return at + [[cand_s[piece * n_cand + 2 * t + half] for half in range(2)]]

    def pair_step(ph, t):
        piece = ph // heads
        head = ph - piece * heads
        q_at = pl.ds(pl.multiple_of(piece * stride + t * 2 * BLOCK, SEL_ROWS), 2 * BLOCK)
        q = qbuf[q_at, pl.ds(pl.multiple_of(head * head_size, head_size), head_size)]
        q0, q1 = q[:BLOCK], q[BLOCK:]
        row = ph * span_blocks + 2 * t
        for half, x in enumerate((q0, q1)):
            qpool[pl.ds(row + half, 1), :] = jnp.sum(x.astype(jnp.float32), axis=0, keepdims=True) * (1.0 / BLOCK)
        rhs = jnp.concatenate(
            [jnp.concatenate([q0, zeros], axis=1), jnp.concatenate([zeros, q1], axis=1)], axis=0
        )
        lhs = jnp.concatenate(
            [
                jnp.concatenate(
                    [kbuf[pl.ds(pl.multiple_of(at * BLOCK, BLOCK), BLOCK), :] for at in both], axis=1
                )
                for both in places(ph, t)
            ],
            axis=0,
        )
        scores = lax.dot_general(lhs, rhs, (((1,), (1,)), ((), ())), preferred_element_type=jnp.float32)
        at = ph * pairs + t
        for slot in range(n_slot):
            part = scores[slot * BLOCK : (slot + 1) * BLOCK]
            top = jnp.max(part, axis=0, keepdims=True)
            ms[at, slot : slot + 1, :] = top
            ss[at, slot : slot + 1, :] = jnp.sum(jnp.exp2((part - top) * exp_scale), axis=0, keepdims=True)

    def head_step(ph, carry):
        for t in range(pairs):
            pair_step(ph, t)
        return carry


    slots = ms.shape[1]
    slot_row = lax.broadcasted_iota(jnp.int32, (slots, 1), 0)

    def combine(ph, t):
        piece = ph // heads
        head = ph - piece * heads
        row = ph * span_blocks + 2 * t
        at = ph * pairs + t
        drop = [sel_s[piece, 2 * t + half, heads * n_sel + head] for half in range(2)]
        keep = slot_row < jnp.where(low, n_slot - drop[0], n_slot - drop[1])
        tops = jnp.where(keep, ms[at], NEG)
        most = jnp.max(tops, axis=0, keepdims=True)
        weight = jnp.where(keep, jnp.exp2((tops - most) * exp_scale) * ss[at], 0.0)
        share = weight / jnp.sum(weight, axis=0, keepdims=True)
        for half in range(2):
            mine = low if half == 0 else jnp.logical_not(low)
            mean = jnp.sum(jnp.where(mine, share, 0.0), axis=1, keepdims=True) * (1.0 / BLOCK)
            column = lv[piece, pl.ds(pl.multiple_of(head * n_sel, n_sel), n_sel), 2 * t + half : 2 * t + half + 1]
            own = jnp.full((slots - n_sel, 1), cand_s[piece * n_cand + 2 * t + half], jnp.int32)
            column = jnp.concatenate([column, own], axis=0)
            for c in range(blocks // LANES):
                hit = column == lane + c * LANES
                teach[c, pl.ds(row + half, 1), :] = jnp.sum(
                    jnp.where(hit, mean, 0.0), axis=0, keepdims=True
                )

    def combine_step(ph, carry):
        for t in range(pairs):
            combine(ph, t)
        head_step(jnp.minimum(ph + 1, n_piece * heads - 1), 0)
        return carry

    head_step(0, 0)
    lax.fori_loop(0, n_piece * heads, combine_step, 0, unroll=14)

    for copy in w_copies:
        copy.wait()
    k_gate = jnp.dot(
        pool[...].astype(jnp.bfloat16), wk_ref[...], preferred_element_type=jnp.float32
    ).astype(jnp.bfloat16)
    q_gate = jnp.dot(
        qpool[...].astype(jnp.bfloat16), wq_ref[...], preferred_element_type=jnp.float32
    ).astype(jnp.bfloat16)
    logits = lax.dot_general(
        q_gate, k_gate, (((1,), (1,)), ((), ())), preferred_element_type=jnp.float32
    ) * (1.0 / math.sqrt(wq_ref.shape[1]))
    top = jnp.max(logits, axis=1, keepdims=True)
    log_gate = logits - top - jnp.log(jnp.sum(jnp.exp(logits - top), axis=1, keepdims=True))
    teacher = jnp.concatenate([teach[c] for c in range(blocks // LANES)], axis=1)
    positive = teacher > 0
    safe = jnp.where(positive, teacher, 1.0)
    kl = jnp.sum(jnp.where(positive, teacher * (jnp.log(safe) - log_gate), 0.0), axis=1, keepdims=True)
    r = lax.broadcasted_iota(jnp.int32, (rows, 1), 0)
    spread = jnp.where(r // span_blocks % heads + cand_s[n_piece * n_cand] == lane, kl, 0.0)
    r = lax.broadcasted_iota(jnp.int32, (1, rows), 1)
    b = lax.broadcasted_iota(jnp.int32, (8 * n_piece, 1), 0)
    pick = (r % span_blocks == b % 8) & (r // (span_blocks * heads) == b // 8)
    tiles = jnp.dot(
        pick.astype(jnp.float32), spread, preferred_element_type=jnp.float32, precision=lax.Precision.HIGHEST
    )
    for i in range(n_piece):
        out_refs[i][...] = tiles[8 * i : 8 * i + 8]


def gate_call(cand, q_plan, q_pieces, k_pieces, w_query, key_gate_weight, stride, heads, n_sel, n_cand):
    head_size = w_query.shape[0]
    span_blocks = (stride - SEL_ROWS) // BLOCK
    n_piece = sum(count for _, _, count, _ in q_plan) // stride
    blocks = sum(x.shape[0] for x in k_pieces) // BLOCK
    rows = n_piece * heads * span_blocks
    dims = (
        tuple(q_plan), n_piece, len(q_pieces), len(k_pieces), heads, n_sel, n_cand, blocks, head_size, stride,
    )
    slots = -(-(n_sel + 1) // 8) * 8
    smem = pl.BlockSpec(memory_space=pltpu.SMEM)
    hbm = pl.BlockSpec(memory_space=pl.ANY)
    vmem = pl.BlockSpec(memory_space=pltpu.VMEM)
    return pl.pallas_call(
        functools.partial(gate_kernel, dims),
        out_shape=[jax.ShapeDtypeStruct((8, LANES), jnp.float32)] * n_piece,
        in_specs=[smem] + [hbm] * (len(q_pieces) + len(k_pieces) + 2),
        out_specs=[vmem] * n_piece,
        scratch_shapes=[
            pltpu.VMEM((n_piece * stride, heads * head_size), jnp.bfloat16),
            pltpu.VMEM((blocks * BLOCK, head_size), jnp.bfloat16),
            pltpu.VMEM((blocks, 3 * head_size), jnp.float32),
            pltpu.VMEM((rows, head_size), jnp.float32),
            pltpu.VMEM((blocks // LANES, rows, LANES), jnp.float32),
            pltpu.VMEM((rows // 2, slots, LANES), jnp.float32),
            pltpu.VMEM((rows // 2, slots, LANES), jnp.float32),
            pltpu.VMEM((n_piece, LANES, LANES), jnp.int32),
            pltpu.VMEM((n_piece, 8, LANES), jnp.int32),
            pltpu.SMEM((n_piece, 8, LANES), jnp.int32),
            pltpu.VMEM(w_query.shape, w_query.dtype),
            pltpu.VMEM(key_gate_weight.shape, key_gate_weight.dtype),
            pltpu.SemaphoreType.DMA((len(q_plan),)),
            pltpu.SemaphoreType.DMA((len(k_pieces),)),
            pltpu.SemaphoreType.DMA(()),
            pltpu.SemaphoreType.DMA((2,)),
        ],
        compiler_params=pltpu.CompilerParams(vmem_limit_bytes=40 * 1024 * 1024),
    )(cand, *q_pieces, *k_pieces, w_query, key_gate_weight)


def per_device(queries, key_state_rows, wanted, selected, w_query, key_gate_weight):
    n_ctx, n_pair = lax.axis_size("ctx"), lax.axis_size("pair")
    ctx, core = lax.axis_index("ctx"), lax.axis_index("pair")
    head_size = w_query.shape[0]
    span, key_width = key_state_rows.shape
    span_blocks = span // BLOCK
    q_heads = queries.shape[1] // head_size
    kv_heads = key_width // head_size
    heads = q_heads // kv_heads
    n_sel = selected.shape[2]
    plane = kv_heads if kv_heads in (1, 2, 4) and n_ctx % kv_heads == 0 and n_pair == 2 else 1
    layers = n_ctx // plane
    ring = plane > 1 and layers <= 4
    spot = ctx % plane
    layer = ctx // plane

    def place_of(block):
        if not ring:
            return block
        span_id = block // span_blocks
        other_ctx = span_id // n_pair
        step = (layer - other_ctx // plane) % layers
        which = (other_ctx % plane) ^ spot
        side = (span_id % n_pair) ^ core
        last = layers - 1
        at = jnp.where(step == last, last * n_pair + side, side * last + step)
        return (at * plane + which) * span_blocks + block % span_blocks

    local_ids = jnp.arange(span_blocks, dtype=jnp.int32)
    candidates = []
    for p in range(plane if ring else 1):
        other_span = (ctx ^ p) * n_pair + core
        wants = lax.dynamic_index_in_dim(wanted, other_span, 0, keepdims=False)
        candidates.append(
            jnp.concatenate(
                [other_span * span_blocks + local_ids, (other_span ^ 1) * span_blocks + local_ids, wants]
            )
        )
    n_cand = candidates[0].shape[0]
    first_lane = spot * heads if ring else 0
    cand = jnp.concatenate(
        [place_of(jnp.concatenate(candidates)).astype(jnp.int32), jnp.full((1,), first_lane, jnp.int32)]
    )

    width = heads * head_size
    stride = span + SEL_ROWS
    sel_rows = jnp.pad(
        selected.astype(jnp.bfloat16).reshape(span_blocks, kv_heads, heads * n_sel),
        ((0, SEL_ROWS - span_blocks), (0, 0), (0, width - heads * n_sel)),
    ).reshape(SEL_ROWS, q_heads * head_size)
    sent = jnp.concatenate([queries, sel_rows], axis=0)
    if not ring:
        gathered = lax.all_gather(key_state_rows, ("ctx", "pair"), axis=0, tiled=True)
        outs = []
        for g in range(kv_heads):
            (out,) = gate_call(
                cand,
                [(0, 0, stride, 0)],
                [sent[:, g * width : (g + 1) * width]],
                [gathered[:, g * head_size : (g + 1) * head_size]],
                w_query, key_gate_weight, stride, heads, n_sel, n_cand,
            )
            outs.append(out[:span_blocks, :heads])
        return jnp.concatenate(outs, axis=1)

    def flipped(x, p):
        return x if p == 0 else lax.ppermute(x, "ctx", [(i, i ^ p) for i in range(n_ctx)])

    def other_core(x):
        return lax.ppermute(x, "pair", [(0, 1), (1, 0)])

    keys = [
        flipped(lax.dynamic_slice_in_dim(key_state_rows, (spot ^ p) * head_size, head_size, 1), p)
        for p in range(plane)
    ]
    parts = [lax.dynamic_slice_in_dim(sent, (spot ^ p) * width, width, 1) for p in range(plane - 1)]
    for first, count in ((0, 64), (64, stride - 64)):
        parts.append(lax.dynamic_slice(sent, (first, (spot ^ (plane - 1)) * width), (count, width)))
    steps = [jnp.concatenate(keys, axis=0)]
    other = []
    steps[0], parts = lax.optimization_barrier((steps[0], parts))
    pieces = [flipped(x, min(p, plane - 1)) for p, x in enumerate(parts)]
    for i in range(layers - 1):
        if i == 2:
            steps[2], pieces[1:4], cand = lax.optimization_barrier((steps[2], pieces[1:4], cand))
        steps.append(lax.ppermute(steps[i], "ctx", [(j, (j + plane) % n_ctx) for j in range(n_ctx)]))
    other += [other_core(x) for x in steps[len(other) :]]
    k_pieces = [jnp.concatenate(steps[:-1] + other[:-1], axis=0), steps[-1], other[-1]]
    q_pieces = pieces
    q_plan, to = [], 0
    for i, x in enumerate(q_pieces):
        q_plan.append((i, 0, x.shape[0], to))
        to += x.shape[0]
    outs = gate_call(
        cand, q_plan, q_pieces, k_pieces, w_query, key_gate_weight, stride, heads, n_sel, n_cand
    )
    back = [flipped(x, p) for p, x in enumerate(outs)]
    return functools.reduce(jnp.add, [x[:span_blocks, :q_heads] for x in back])


def solution(mesh):
    return jax.shard_map(
        per_device,
        mesh=mesh,
        in_specs=(
            P(("groups", "ctx", "pair"), "head"),
            P(("groups", "ctx", "pair"), "head"),
            P("groups", None),
            P(("groups", "ctx", "pair"), "head", None),
            P(),
            P(),
        ),
        out_specs=P(("groups", "ctx", "pair"), "head"),
        check_vma=False,
    )
```

```python
import functools
import math

import jax
import jax.numpy as jnp
from jax import lax
from jax.experimental import pallas as pl
from jax.experimental.pallas import tpu as pltpu
from jax.sharding import PartitionSpec as P

BLOCK = 64
LANES = 128
SEL_ROWS = 16
NEG = -1e37


def gate_kernel(dims, *refs):
    q_plan, n_piece, n_q, n_key, heads, n_sel, n_cand, blocks, head_size, stride = dims
    cand_s = refs[0]
    q_in = refs[1 : 1 + n_q]
    k_in = refs[1 + n_q : 1 + n_q + n_key]
    refs = refs[1 + n_q + n_key :]
    wq_in, wk_in = refs[:2]
    out_refs = refs[2 : 2 + n_piece]
    qbuf, kbuf, pool, qpool, teach, ms, ss, lv, sel_v, sel_s, wq_ref, wk_ref, sem_q, sem_k, sem_s, sem_w = refs[2 + n_piece :]
    span = stride - SEL_ROWS
    span_blocks = span // BLOCK
    n_slot = n_sel + 1
    rows = n_piece * heads * span_blocks
    exp_scale = math.log2(math.e) / math.sqrt(head_size)

    q_copies = [
        pltpu.make_async_copy(q_in[src].at[pl.ds(row, count)], qbuf.at[pl.ds(to, count)], sem_q.at[i])
        for i, (src, row, count, to) in enumerate(q_plan)
    ]
    k_copies, to = [], 0
    for i, k in enumerate(k_in):
        k_copies.append(pltpu.make_async_copy(k, kbuf.at[pl.ds(to, k.shape[0])], sem_k.at[i]))
        to += k.shape[0]
    w_copies = [
        pltpu.make_async_copy(wq_in, wq_ref, sem_w.at[0]),
        pltpu.make_async_copy(wk_in, wk_ref, sem_w.at[1]),
    ]
    for copy in q_copies + k_copies + w_copies:
        copy.start()
    for copy in q_copies:
        copy.wait()

    lane = lax.broadcasted_iota(jnp.int32, (1, LANES), 1)
    sub = lax.broadcasted_iota(jnp.int32, (8, 1), 0)
    listed = lane < heads * n_sel
    group = lax.broadcasted_iota(jnp.int32, (LANES, 1), 0) // n_sel + heads * n_sel == lane
    for i in range(n_piece):
        mine = qbuf[i * stride + span : (i + 1) * stride, :LANES].astype(jnp.float32)[:8].astype(jnp.int32)
        own = ((mine == sub) & listed).astype(jnp.float32).astype(jnp.bfloat16)
        own = jnp.dot(own, group.astype(jnp.float32).astype(jnp.bfloat16), preferred_element_type=jnp.float32)
        at = own.astype(jnp.int32)
        for m in range(n_cand):
            at = jnp.where((mine == m) & listed, cand_s[i * n_cand + m], at)
        sel_v[i] = at
        lv[i] = jnp.transpose(jnp.broadcast_to(at.astype(jnp.float32)[None], (LANES // 8, 8, LANES)).reshape(LANES, LANES)).astype(jnp.int32)
    sel_copy = pltpu.make_async_copy(sel_v, sel_s, sem_s)
    sel_copy.start()
    for copy in k_copies:
        copy.wait()

    def pool_step(i, carry):
        first = pl.multiple_of(i * 8 * BLOCK, 8 * BLOCK)
        keys = kbuf[pl.ds(first, 8 * BLOCK), :].astype(jnp.float32).reshape(8, BLOCK, head_size)
        at = pl.ds(pl.multiple_of(i * 8, 8), 8)
        pool[at, 0:head_size] = jnp.max(keys, axis=1)
        pool[at, head_size : 2 * head_size] = jnp.min(keys, axis=1)
        pool[at, 2 * head_size :] = jnp.sum(keys, axis=1) * (1.0 / BLOCK)
        return carry

    lax.fori_loop(0, blocks // 8, pool_step, 0)
    sel_copy.wait()

    low = lane < BLOCK
    zeros = jnp.zeros((BLOCK, head_size), jnp.bfloat16)
    pairs = span_blocks // 2

    def places(ph, t):
        piece = ph // heads
        head = ph - piece * heads
        at = [
            [sel_s[piece, 2 * t + half, head * n_sel + slot] for half in range(2)] for slot in range(n_sel)
        ]
        return at + [[cand_s[piece * n_cand + 2 * t + half] for half in range(2)]]

    def pair_step(ph, t):
        piece = ph // heads
        head = ph - piece * heads
        q_at = pl.ds(pl.multiple_of(piece * stride + t * 2 * BLOCK, SEL_ROWS), 2 * BLOCK)
        q = qbuf[q_at, pl.ds(pl.multiple_of(head * head_size, head_size), head_size)]
        q0, q1 = q[:BLOCK], q[BLOCK:]
        row = ph * span_blocks + 2 * t
        for half, x in enumerate((q0, q1)):
            qpool[pl.ds(row + half, 1), :] = jnp.sum(x.astype(jnp.float32), axis=0, keepdims=True) * (1.0 / BLOCK)
        rhs = jnp.concatenate(
            [jnp.concatenate([q0, zeros], axis=1), jnp.concatenate([zeros, q1], axis=1)], axis=0
        )
        lhs = jnp.concatenate(
            [
                jnp.concatenate(
                    [kbuf[pl.ds(pl.multiple_of(at * BLOCK, BLOCK), BLOCK), :] for at in both], axis=1
                )
                for both in places(ph, t)
            ],
            axis=0,
        )
        scores = lax.dot_general(lhs, rhs, (((1,), (1,)), ((), ())), preferred_element_type=jnp.float32)
        at = ph * pairs + t
        for slot in range(n_slot):
            part = scores[slot * BLOCK : (slot + 1) * BLOCK]
            top = jnp.max(part, axis=0, keepdims=True)
            ms[at, slot : slot + 1, :] = top
            ss[at, slot : slot + 1, :] = jnp.sum(jnp.exp2((part - top) * exp_scale), axis=0, keepdims=True)

    def head_step(ph, carry):
        for t in range(pairs):
            pair_step(ph, t)
        return carry


    slots = ms.shape[1]
    slot_row = lax.broadcasted_iota(jnp.int32, (slots, 1), 0)

    def combine(ph, t):
        piece = ph // heads
        head = ph - piece * heads
        row = ph * span_blocks + 2 * t
        at = ph * pairs + t
        drop = [sel_s[piece, 2 * t + half, heads * n_sel + head] for half in range(2)]
        keep = slot_row < jnp.where(low, n_slot - drop[0], n_slot - drop[1])
        tops = jnp.where(keep, ms[at], NEG)
        most = jnp.max(tops, axis=0, keepdims=True)
        weight = jnp.where(keep, jnp.exp2((tops - most) * exp_scale) * ss[at], 0.0)
        share = weight / jnp.sum(weight, axis=0, keepdims=True)
        for half in range(2):
            mine = low if half == 0 else jnp.logical_not(low)
            mean = jnp.sum(jnp.where(mine, share, 0.0), axis=1, keepdims=True) * (1.0 / BLOCK)
            column = lv[piece, pl.ds(pl.multiple_of(head * n_sel, n_sel), n_sel), 2 * t + half : 2 * t + half + 1]
            own = jnp.full((slots - n_sel, 1), cand_s[piece * n_cand + 2 * t + half], jnp.int32)
            column = jnp.concatenate([column, own], axis=0)
            for c in range(blocks // LANES):
                hit = column == lane + c * LANES
                teach[c, pl.ds(row + half, 1), :] = jnp.sum(
                    jnp.where(hit, mean, 0.0), axis=0, keepdims=True
                )

    def combine_step(ph, carry):
        for t in range(pairs):
            combine(ph, t)
        head_step(jnp.minimum(ph + 1, n_piece * heads - 1), 0)
        return carry

    head_step(0, 0)
    lax.fori_loop(0, n_piece * heads, combine_step, 0, unroll=28)

    for copy in w_copies:
        copy.wait()
    k_gate = jnp.dot(
        pool[...].astype(jnp.bfloat16), wk_ref[...], preferred_element_type=jnp.float32
    ).astype(jnp.bfloat16)
    q_gate = jnp.dot(
        qpool[...].astype(jnp.bfloat16), wq_ref[...], preferred_element_type=jnp.float32
    ).astype(jnp.bfloat16)
    logits = lax.dot_general(
        q_gate, k_gate, (((1,), (1,)), ((), ())), preferred_element_type=jnp.float32
    ) * (1.0 / math.sqrt(wq_ref.shape[1]))
    top = jnp.max(logits, axis=1, keepdims=True)
    log_gate = logits - top - jnp.log(jnp.sum(jnp.exp(logits - top), axis=1, keepdims=True))
    teacher = jnp.concatenate([teach[c] for c in range(blocks // LANES)], axis=1)
    positive = teacher > 0
    safe = jnp.where(positive, teacher, 1.0)
    kl = jnp.sum(jnp.where(positive, teacher * (jnp.log(safe) - log_gate), 0.0), axis=1, keepdims=True)
    r = lax.broadcasted_iota(jnp.int32, (rows, 1), 0)
    spread = jnp.where(r // span_blocks % heads + cand_s[n_piece * n_cand] == lane, kl, 0.0)
    r = lax.broadcasted_iota(jnp.int32, (1, rows), 1)
    b = lax.broadcasted_iota(jnp.int32, (8 * n_piece, 1), 0)
    pick = (r % span_blocks == b % 8) & (r // (span_blocks * heads) == b // 8)
    tiles = jnp.dot(
        pick.astype(jnp.float32), spread, preferred_element_type=jnp.float32, precision=lax.Precision.HIGHEST
    )
    for i in range(n_piece):
        out_refs[i][...] = tiles[8 * i : 8 * i + 8]


def gate_call(cand, q_plan, q_pieces, k_pieces, w_query, key_gate_weight, stride, heads, n_sel, n_cand):
    head_size = w_query.shape[0]
    span_blocks = (stride - SEL_ROWS) // BLOCK
    n_piece = sum(count for _, _, count, _ in q_plan) // stride
    blocks = sum(x.shape[0] for x in k_pieces) // BLOCK
    rows = n_piece * heads * span_blocks
    dims = (
        tuple(q_plan), n_piece, len(q_pieces), len(k_pieces), heads, n_sel, n_cand, blocks, head_size, stride,
    )
    slots = -(-(n_sel + 1) // 8) * 8
    smem = pl.BlockSpec(memory_space=pltpu.SMEM)
    hbm = pl.BlockSpec(memory_space=pl.ANY)
    vmem = pl.BlockSpec(memory_space=pltpu.VMEM)
    return pl.pallas_call(
        functools.partial(gate_kernel, dims),
        out_shape=[jax.ShapeDtypeStruct((8, LANES), jnp.float32)] * n_piece,
        in_specs=[smem] + [hbm] * (len(q_pieces) + len(k_pieces) + 2),
        out_specs=[vmem] * n_piece,
        scratch_shapes=[
            pltpu.VMEM((n_piece * stride, heads * head_size), jnp.bfloat16),
            pltpu.VMEM((blocks * BLOCK, head_size), jnp.bfloat16),
            pltpu.VMEM((blocks, 3 * head_size), jnp.float32),
            pltpu.VMEM((rows, head_size), jnp.float32),
            pltpu.VMEM((blocks // LANES, rows, LANES), jnp.float32),
            pltpu.VMEM((rows // 2, slots, LANES), jnp.float32),
            pltpu.VMEM((rows // 2, slots, LANES), jnp.float32),
            pltpu.VMEM((n_piece, LANES, LANES), jnp.int32),
            pltpu.VMEM((n_piece, 8, LANES), jnp.int32),
            pltpu.SMEM((n_piece, 8, LANES), jnp.int32),
            pltpu.VMEM(w_query.shape, w_query.dtype),
            pltpu.VMEM(key_gate_weight.shape, key_gate_weight.dtype),
            pltpu.SemaphoreType.DMA((len(q_plan),)),
            pltpu.SemaphoreType.DMA((len(k_pieces),)),
            pltpu.SemaphoreType.DMA(()),
            pltpu.SemaphoreType.DMA((2,)),
        ],
        compiler_params=pltpu.CompilerParams(vmem_limit_bytes=40 * 1024 * 1024),
    )(cand, *q_pieces, *k_pieces, w_query, key_gate_weight)


def per_device(queries, key_state_rows, wanted, selected, w_query, key_gate_weight):
    n_ctx, n_pair = lax.axis_size("ctx"), lax.axis_size("pair")
    ctx, core = lax.axis_index("ctx"), lax.axis_index("pair")
    head_size = w_query.shape[0]
    span, key_width = key_state_rows.shape
    span_blocks = span // BLOCK
    q_heads = queries.shape[1] // head_size
    kv_heads = key_width // head_size
    heads = q_heads // kv_heads
    n_sel = selected.shape[2]
    plane = kv_heads if kv_heads in (1, 2, 4) and n_ctx % kv_heads == 0 and n_pair == 2 else 1
    layers = n_ctx // plane
    ring = plane > 1 and layers <= 4
    spot = ctx % plane
    layer = ctx // plane

    def place_of(block):
        if not ring:
            return block
        span_id = block // span_blocks
        other_ctx = span_id // n_pair
        step = (layer - other_ctx // plane) % layers
        which = (other_ctx % plane) ^ spot
        side = (span_id % n_pair) ^ core
        last = layers - 1
        at = jnp.where(step == last, last * n_pair + side, side * last + step)
        return (at * plane + which) * span_blocks + block % span_blocks

    local_ids = jnp.arange(span_blocks, dtype=jnp.int32)
    candidates = []
    for p in range(plane if ring else 1):
        other_span = (ctx ^ p) * n_pair + core
        wants = lax.dynamic_index_in_dim(wanted, other_span, 0, keepdims=False)
        candidates.append(
            jnp.concatenate(
                [other_span * span_blocks + local_ids, (other_span ^ 1) * span_blocks + local_ids, wants]
            )
        )
    n_cand = candidates[0].shape[0]
    first_lane = spot * heads if ring else 0
    cand = jnp.concatenate(
        [place_of(jnp.concatenate(candidates)).astype(jnp.int32), jnp.full((1,), first_lane, jnp.int32)]
    )

    width = heads * head_size
    stride = span + SEL_ROWS
    sel_rows = jnp.pad(
        selected.astype(jnp.bfloat16).reshape(span_blocks, kv_heads, heads * n_sel),
        ((0, SEL_ROWS - span_blocks), (0, 0), (0, width - heads * n_sel)),
    ).reshape(SEL_ROWS, q_heads * head_size)
    sent = jnp.concatenate([queries, sel_rows], axis=0)
    if not ring:
        gathered = lax.all_gather(key_state_rows, ("ctx", "pair"), axis=0, tiled=True)
        outs = []
        for g in range(kv_heads):
            (out,) = gate_call(
                cand,
                [(0, 0, stride, 0)],
                [sent[:, g * width : (g + 1) * width]],
                [gathered[:, g * head_size : (g + 1) * head_size]],
                w_query, key_gate_weight, stride, heads, n_sel, n_cand,
            )
            outs.append(out[:span_blocks, :heads])
        return jnp.concatenate(outs, axis=1)

    def flipped(x, p):
        return x if p == 0 else lax.ppermute(x, "ctx", [(i, i ^ p) for i in range(n_ctx)])

    def other_core(x):
        return lax.ppermute(x, "pair", [(0, 1), (1, 0)])

    keys = [
        flipped(lax.dynamic_slice_in_dim(key_state_rows, (spot ^ p) * head_size, head_size, 1), p)
        for p in range(plane)
    ]
    parts = [lax.dynamic_slice_in_dim(sent, (spot ^ p) * width, width, 1) for p in range(plane - 1)]
    for first, count in ((0, 64), (64, stride - 64)):
        parts.append(lax.dynamic_slice(sent, (first, (spot ^ (plane - 1)) * width), (count, width)))
    steps = [jnp.concatenate(keys, axis=0)]
    other = []
    steps[0], parts = lax.optimization_barrier((steps[0], parts))
    pieces = [flipped(x, min(p, plane - 1)) for p, x in enumerate(parts)]
    for i in range(layers - 1):
        if i == 2:
            steps[2], pieces[1:4], cand = lax.optimization_barrier((steps[2], pieces[1:4], cand))
        steps.append(lax.ppermute(steps[i], "ctx", [(j, (j + plane) % n_ctx) for j in range(n_ctx)]))
    other += [other_core(x) for x in steps[len(other) :]]
    k_pieces = [jnp.concatenate(steps[:-1] + other[:-1], axis=0), steps[-1], other[-1]]
    q_pieces = pieces
    q_plan, to = [], 0
    for i, x in enumerate(q_pieces):
        q_plan.append((i, 0, x.shape[0], to))
        to += x.shape[0]
    outs = gate_call(
        cand, q_plan, q_pieces, k_pieces, w_query, key_gate_weight, stride, heads, n_sel, n_cand
    )
    back = [flipped(x, p) for p, x in enumerate(outs)]
    return functools.reduce(jnp.add, [x[:span_blocks, :q_heads] for x in back])


def solution(mesh):
    return jax.shard_map(
        per_device,
        mesh=mesh,
        in_specs=(
            P(("groups", "ctx", "pair"), "head"),
            P(("groups", "ctx", "pair"), "head"),
            P("groups", None),
            P(("groups", "ctx", "pair"), "head", None),
            P(),
            P(),
        ),
        out_specs=P(("groups", "ctx", "pair"), "head"),
        check_vma=False,
    )
```

```python
import functools
import math

import jax
import jax.numpy as jnp
from jax import lax
from jax.experimental import pallas as pl
from jax.experimental.pallas import tpu as pltpu
from jax.sharding import PartitionSpec as P

BLOCK = 64
LANES = 128
SEL_ROWS = 16
NEG = -1e37


def gate_kernel(dims, *refs):
    q_plan, n_piece, n_q, n_key, heads, n_sel, n_cand, blocks, head_size, stride = dims
    cand_s = refs[0]
    q_in = refs[1 : 1 + n_q]
    k_in = refs[1 + n_q : 1 + n_q + n_key]
    refs = refs[1 + n_q + n_key :]
    wq_in, wk_in = refs[:2]
    out_refs = refs[2 : 2 + n_piece]
    qbuf, kbuf, pool, qpool, teach, ms, ss, lv, sel_v, sel_s, wq_ref, wk_ref, sem_q, sem_k, sem_s, sem_w = refs[2 + n_piece :]
    span = stride - SEL_ROWS
    span_blocks = span // BLOCK
    n_slot = n_sel + 1
    rows = n_piece * heads * span_blocks
    exp_scale = math.log2(math.e) / math.sqrt(head_size)

    q_copies = [
        pltpu.make_async_copy(q_in[src].at[pl.ds(row, count)], qbuf.at[pl.ds(to, count)], sem_q.at[i])
        for i, (src, row, count, to) in enumerate(q_plan)
    ]
    k_copies, to = [], 0
    for i, k in enumerate(k_in):
        k_copies.append(pltpu.make_async_copy(k, kbuf.at[pl.ds(to, k.shape[0])], sem_k.at[i]))
        to += k.shape[0]
    w_copies = [
        pltpu.make_async_copy(wq_in, wq_ref, sem_w.at[0]),
        pltpu.make_async_copy(wk_in, wk_ref, sem_w.at[1]),
    ]
    for copy in q_copies + k_copies + w_copies:
        copy.start()
    for copy in q_copies:
        copy.wait()

    lane = lax.broadcasted_iota(jnp.int32, (1, LANES), 1)
    sub = lax.broadcasted_iota(jnp.int32, (8, 1), 0)
    listed = lane < heads * n_sel
    group = lax.broadcasted_iota(jnp.int32, (LANES, 1), 0) // n_sel + heads * n_sel == lane
    for i in range(n_piece):
        mine = qbuf[i * stride + span : (i + 1) * stride, :LANES].astype(jnp.float32)[:8].astype(jnp.int32)
        own = ((mine == sub) & listed).astype(jnp.float32).astype(jnp.bfloat16)
        own = jnp.dot(own, group.astype(jnp.float32).astype(jnp.bfloat16), preferred_element_type=jnp.float32)
        at = own.astype(jnp.int32)
        for m in range(n_cand):
            at = jnp.where((mine == m) & listed, cand_s[i * n_cand + m], at)
        sel_v[i] = at
        lv[i] = jnp.transpose(jnp.broadcast_to(at.astype(jnp.float32)[None], (LANES // 8, 8, LANES)).reshape(LANES, LANES)).astype(jnp.int32)
    sel_copy = pltpu.make_async_copy(sel_v, sel_s, sem_s)
    sel_copy.start()
    for copy in k_copies:
        copy.wait()

    def pool_step(i, carry):
        first = pl.multiple_of(i * 8 * BLOCK, 8 * BLOCK)
        keys = kbuf[pl.ds(first, 8 * BLOCK), :].astype(jnp.float32).reshape(8, BLOCK, head_size)
        at = pl.ds(pl.multiple_of(i * 8, 8), 8)
        pool[at, 0:head_size] = jnp.max(keys, axis=1)
        pool[at, head_size : 2 * head_size] = jnp.min(keys, axis=1)
        pool[at, 2 * head_size :] = jnp.sum(keys, axis=1) * (1.0 / BLOCK)
        return carry

    lax.fori_loop(0, blocks // 8, pool_step, 0)
    sel_copy.wait()

    low = lane < BLOCK
    zeros = jnp.zeros((BLOCK, head_size), jnp.bfloat16)
    pairs = span_blocks // 2

    def places(ph, t):
        piece = ph // heads
        head = ph - piece * heads
        at = [
            [sel_s[piece, 2 * t + half, head * n_sel + slot] for half in range(2)] for slot in range(n_sel)
        ]
        return at + [[cand_s[piece * n_cand + 2 * t + half] for half in range(2)]]

    def pair_step(ph, t):
        piece = ph // heads
        head = ph - piece * heads
        q_at = pl.ds(pl.multiple_of(piece * stride + t * 2 * BLOCK, SEL_ROWS), 2 * BLOCK)
        q = qbuf[q_at, pl.ds(pl.multiple_of(head * head_size, head_size), head_size)]
        q0, q1 = q[:BLOCK], q[BLOCK:]
        row = ph * span_blocks + 2 * t
        for half, x in enumerate((q0, q1)):
            qpool[pl.ds(row + half, 1), :] = jnp.sum(x.astype(jnp.float32), axis=0, keepdims=True) * (1.0 / BLOCK)
        rhs = jnp.concatenate(
            [jnp.concatenate([q0, zeros], axis=1), jnp.concatenate([zeros, q1], axis=1)], axis=0
        )
        lhs = jnp.concatenate(
            [
                jnp.concatenate(
                    [kbuf[pl.ds(pl.multiple_of(at * BLOCK, BLOCK), BLOCK), :] for at in both], axis=1
                )
                for both in places(ph, t)
            ],
            axis=0,
        )
        scores = lax.dot_general(lhs, rhs, (((1,), (1,)), ((), ())), preferred_element_type=jnp.float32)
        at = ph * pairs + t
        for slot in range(n_slot):
            part = scores[slot * BLOCK : (slot + 1) * BLOCK]
            top = jnp.max(part, axis=0, keepdims=True)
            ms[at, slot : slot + 1, :] = top
            ss[at, slot : slot + 1, :] = jnp.sum(jnp.exp2((part - top) * exp_scale), axis=0, keepdims=True)

    def head_step(ph, carry):
        for t in range(pairs):
            pair_step(ph, t)
        return carry


    slots = ms.shape[1]
    slot_row = lax.broadcasted_iota(jnp.int32, (slots, 1), 0)

    def combine(ph, t):
        piece = ph // heads
        head = ph - piece * heads
        row = ph * span_blocks + 2 * t
        at = ph * pairs + t
        drop = [sel_s[piece, 2 * t + half, heads * n_sel + head] for half in range(2)]
        keep = slot_row < jnp.where(low, n_slot - drop[0], n_slot - drop[1])
        tops = jnp.where(keep, ms[at], NEG)
        most = jnp.max(tops, axis=0, keepdims=True)
        weight = jnp.where(keep, jnp.exp2((tops - most) * exp_scale) * ss[at], 0.0)
        share = weight / jnp.sum(weight, axis=0, keepdims=True)
        for half in range(2):
            mine = low if half == 0 else jnp.logical_not(low)
            mean = jnp.sum(jnp.where(mine, share, 0.0), axis=1, keepdims=True) * (1.0 / BLOCK)
            column = lv[piece, pl.ds(pl.multiple_of(head * n_sel, n_sel), n_sel), 2 * t + half : 2 * t + half + 1]
            own = jnp.full((slots - n_sel, 1), cand_s[piece * n_cand + 2 * t + half], jnp.int32)
            column = jnp.concatenate([column, own], axis=0)
            for c in range(blocks // LANES):
                hit = column == lane + c * LANES
                teach[c, pl.ds(row + half, 1), :] = jnp.sum(
                    jnp.where(hit, mean, 0.0), axis=0, keepdims=True
                )

    def combine_step(ph, carry):
        for t in range(pairs):
            combine(ph, t)
        head_step(ph + 1, 0)
        return carry

    head_step(0, 0)
    last = n_piece * heads - 1
    lax.fori_loop(0, last, combine_step, 0, unroll=last)
    for t in range(pairs):
        combine(last, t)

    for copy in w_copies:
        copy.wait()
    k_gate = jnp.dot(
        pool[...].astype(jnp.bfloat16), wk_ref[...], preferred_element_type=jnp.float32
    ).astype(jnp.bfloat16)
    q_gate = jnp.dot(
        qpool[...].astype(jnp.bfloat16), wq_ref[...], preferred_element_type=jnp.float32
    ).astype(jnp.bfloat16)
    logits = lax.dot_general(
        q_gate, k_gate, (((1,), (1,)), ((), ())), preferred_element_type=jnp.float32
    ) * (1.0 / math.sqrt(wq_ref.shape[1]))
    top = jnp.max(logits, axis=1, keepdims=True)
    log_gate = logits - top - jnp.log(jnp.sum(jnp.exp(logits - top), axis=1, keepdims=True))
    teacher = jnp.concatenate([teach[c] for c in range(blocks // LANES)], axis=1)
    positive = teacher > 0
    safe = jnp.where(positive, teacher, 1.0)
    kl = jnp.sum(jnp.where(positive, teacher * (jnp.log(safe) - log_gate), 0.0), axis=1, keepdims=True)
    r = lax.broadcasted_iota(jnp.int32, (rows, 1), 0)
    spread = jnp.where(r // span_blocks % heads + cand_s[n_piece * n_cand] == lane, kl, 0.0)
    r = lax.broadcasted_iota(jnp.int32, (1, rows), 1)
    b = lax.broadcasted_iota(jnp.int32, (8 * n_piece, 1), 0)
    pick = (r % span_blocks == b % 8) & (r // (span_blocks * heads) == b // 8)
    tiles = jnp.dot(
        pick.astype(jnp.float32), spread, preferred_element_type=jnp.float32, precision=lax.Precision.HIGHEST
    )
    for i in range(n_piece):
        out_refs[i][...] = tiles[8 * i : 8 * i + 8]


def gate_call(cand, q_plan, q_pieces, k_pieces, w_query, key_gate_weight, stride, heads, n_sel, n_cand):
    head_size = w_query.shape[0]
    span_blocks = (stride - SEL_ROWS) // BLOCK
    n_piece = sum(count for _, _, count, _ in q_plan) // stride
    blocks = sum(x.shape[0] for x in k_pieces) // BLOCK
    rows = n_piece * heads * span_blocks
    dims = (
        tuple(q_plan), n_piece, len(q_pieces), len(k_pieces), heads, n_sel, n_cand, blocks, head_size, stride,
    )
    slots = -(-(n_sel + 1) // 8) * 8
    smem = pl.BlockSpec(memory_space=pltpu.SMEM)
    hbm = pl.BlockSpec(memory_space=pl.ANY)
    vmem = pl.BlockSpec(memory_space=pltpu.VMEM)
    return pl.pallas_call(
        functools.partial(gate_kernel, dims),
        out_shape=[jax.ShapeDtypeStruct((8, LANES), jnp.float32)] * n_piece,
        in_specs=[smem] + [hbm] * (len(q_pieces) + len(k_pieces) + 2),
        out_specs=[vmem] * n_piece,
        scratch_shapes=[
            pltpu.VMEM((n_piece * stride, heads * head_size), jnp.bfloat16),
            pltpu.VMEM((blocks * BLOCK, head_size), jnp.bfloat16),
            pltpu.VMEM((blocks, 3 * head_size), jnp.float32),
            pltpu.VMEM((rows, head_size), jnp.float32),
            pltpu.VMEM((blocks // LANES, rows, LANES), jnp.float32),
            pltpu.VMEM((rows // 2, slots, LANES), jnp.float32),
            pltpu.VMEM((rows // 2, slots, LANES), jnp.float32),
            pltpu.VMEM((n_piece, LANES, LANES), jnp.int32),
            pltpu.VMEM((n_piece, 8, LANES), jnp.int32),
            pltpu.SMEM((n_piece, 8, LANES), jnp.int32),
            pltpu.VMEM(w_query.shape, w_query.dtype),
            pltpu.VMEM(key_gate_weight.shape, key_gate_weight.dtype),
            pltpu.SemaphoreType.DMA((len(q_plan),)),
            pltpu.SemaphoreType.DMA((len(k_pieces),)),
            pltpu.SemaphoreType.DMA(()),
            pltpu.SemaphoreType.DMA((2,)),
        ],
        compiler_params=pltpu.CompilerParams(vmem_limit_bytes=40 * 1024 * 1024),
    )(cand, *q_pieces, *k_pieces, w_query, key_gate_weight)


def per_device(queries, key_state_rows, wanted, selected, w_query, key_gate_weight):
    n_ctx, n_pair = lax.axis_size("ctx"), lax.axis_size("pair")
    ctx, core = lax.axis_index("ctx"), lax.axis_index("pair")
    head_size = w_query.shape[0]
    span, key_width = key_state_rows.shape
    span_blocks = span // BLOCK
    q_heads = queries.shape[1] // head_size
    kv_heads = key_width // head_size
    heads = q_heads // kv_heads
    n_sel = selected.shape[2]
    plane = kv_heads if kv_heads in (1, 2, 4) and n_ctx % kv_heads == 0 and n_pair == 2 else 1
    layers = n_ctx // plane
    ring = plane > 1 and layers <= 4
    spot = ctx % plane
    layer = ctx // plane

    def place_of(block):
        if not ring:
            return block
        span_id = block // span_blocks
        other_ctx = span_id // n_pair
        step = (layer - other_ctx // plane) % layers
        which = (other_ctx % plane) ^ spot
        side = (span_id % n_pair) ^ core
        last = layers - 1
        at = jnp.where(step == last, last * n_pair + side, side * last + step)
        return (at * plane + which) * span_blocks + block % span_blocks

    local_ids = jnp.arange(span_blocks, dtype=jnp.int32)
    candidates = []
    for p in range(plane if ring else 1):
        other_span = (ctx ^ p) * n_pair + core
        wants = lax.dynamic_index_in_dim(wanted, other_span, 0, keepdims=False)
        candidates.append(
            jnp.concatenate(
                [other_span * span_blocks + local_ids, (other_span ^ 1) * span_blocks + local_ids, wants]
            )
        )
    n_cand = candidates[0].shape[0]
    first_lane = spot * heads if ring else 0
    cand = jnp.concatenate(
        [place_of(jnp.concatenate(candidates)).astype(jnp.int32), jnp.full((1,), first_lane, jnp.int32)]
    )

    width = heads * head_size
    stride = span + SEL_ROWS
    sel_rows = jnp.pad(
        selected.astype(jnp.bfloat16).reshape(span_blocks, kv_heads, heads * n_sel),
        ((0, SEL_ROWS - span_blocks), (0, 0), (0, width - heads * n_sel)),
    ).reshape(SEL_ROWS, q_heads * head_size)
    sent = jnp.concatenate([queries, sel_rows], axis=0)
    if not ring:
        gathered = lax.all_gather(key_state_rows, ("ctx", "pair"), axis=0, tiled=True)
        outs = []
        for g in range(kv_heads):
            (out,) = gate_call(
                cand,
                [(0, 0, stride, 0)],
                [sent[:, g * width : (g + 1) * width]],
                [gathered[:, g * head_size : (g + 1) * head_size]],
                w_query, key_gate_weight, stride, heads, n_sel, n_cand,
            )
            outs.append(out[:span_blocks, :heads])
        return jnp.concatenate(outs, axis=1)

    def flipped(x, p):
        return x if p == 0 else lax.ppermute(x, "ctx", [(i, i ^ p) for i in range(n_ctx)])

    def other_core(x):
        return lax.ppermute(x, "pair", [(0, 1), (1, 0)])

    keys = [
        flipped(lax.dynamic_slice_in_dim(key_state_rows, (spot ^ p) * head_size, head_size, 1), p)
        for p in range(plane)
    ]
    parts = [lax.dynamic_slice_in_dim(sent, (spot ^ p) * width, width, 1) for p in range(plane - 1)]
    for first, count in ((0, 64), (64, stride - 64)):
        parts.append(lax.dynamic_slice(sent, (first, (spot ^ (plane - 1)) * width), (count, width)))
    steps = [jnp.concatenate(keys, axis=0)]
    other = []
    steps[0], parts = lax.optimization_barrier((steps[0], parts))
    pieces = [flipped(x, min(p, plane - 1)) for p, x in enumerate(parts)]
    for i in range(layers - 1):
        if i == 2:
            steps[2], pieces[1:4], cand = lax.optimization_barrier((steps[2], pieces[1:4], cand))
        steps.append(lax.ppermute(steps[i], "ctx", [(j, (j + plane) % n_ctx) for j in range(n_ctx)]))
    other += [other_core(x) for x in steps[len(other) :]]
    k_pieces = [jnp.concatenate(steps[:-1] + other[:-1], axis=0), steps[-1], other[-1]]
    q_pieces = pieces
    q_plan, to = [], 0
    for i, x in enumerate(q_pieces):
        q_plan.append((i, 0, x.shape[0], to))
        to += x.shape[0]
    outs = gate_call(
        cand, q_plan, q_pieces, k_pieces, w_query, key_gate_weight, stride, heads, n_sel, n_cand
    )
    back = [flipped(x, p) for p, x in enumerate(outs)]
    return functools.reduce(jnp.add, [x[:span_blocks, :q_heads] for x in back])


def solution(mesh):
    return jax.shard_map(
        per_device,
        mesh=mesh,
        in_specs=(
            P(("groups", "ctx", "pair"), "head"),
            P(("groups", "ctx", "pair"), "head"),
            P("groups", None),
            P(("groups", "ctx", "pair"), "head", None),
            P(),
            P(),
        ),
        out_specs=P(("groups", "ctx", "pair"), "head"),
        check_vma=False,
    )
```
